32 devices in a mesh: seq: 16 (over z, y, x), head: 2 (over core).
Axes of the slice: x: 2, y: 2, z: 4, core: 2. Of those that a mesh axis runs over, the one named last changes fastest.
Arguments:
- queries: bfloat16 [8192, 4096], P('seq', 'head'), may hold values from -10 to 10
- keys: bfloat16 [8192, 4096], P('seq', 'head'), may hold values from -4.5 to 7
- values: bfloat16 [8192, 4096], P('seq', 'head'), may hold values from -8 to 8
- gate_bias: float32 [32], P('head'), may hold values from -3 to 3
- out_weight: bfloat16 [4096, 4096], P('head'), may hold values from -0.09375 to 0.09375
Outputs:
- mixed: bfloat16 [8192, 4096], P(('seq', 'head'))
The draws below stay inside these ranges and needn't reach their ends.
All inputs are finite; a program needn't handle non-finite values.
Results may differ from the reference program's by a relative error of at most 0.004.
The reference program's roundings to bfloat16 on the way count: a program that leaves them out, or rounds other values in their place, can miss the bound.
Values sent between devices are 32-bit elements; how exact they have to be, the bound alone decides.
A program may use at most 256 MiB of HBM per device.

```python
import jax
import jax.numpy as jnp
from jax import lax

H = 32
DH = 128
D = 4096
SEG = 512
TOKENS = 8192


def lifted_draw(source):
    return jnp.where(source > 0, source + 1.0, jnp.exp(jnp.minimum(source, 0.0)))


def sparse_field(noise_key, mask_key, level_key, arr_shape):
    active = jax.random.uniform(mask_key, arr_shape, jnp.float32) < 4.0 / DH
    quiet_part = jnp.clip(-3.0 + 0.3 * jax.random.normal(noise_key, arr_shape, jnp.float32), -4.5, -1.5)
    loud_part = jax.random.uniform(level_key, arr_shape, jnp.float32, 2.0, 7.0)
    return jnp.where(active, loud_part, quiet_part)


def paired_draw(key):
    arr_shape = (TOKENS, H * DH)
    query_arr = sparse_field(jax.random.fold_in(key, 11), jax.random.fold_in(key, 13), jax.random.fold_in(key, 15), arr_shape)
    key_arr = sparse_field(jax.random.fold_in(key, 12), jax.random.fold_in(key, 14), jax.random.fold_in(key, 16), arr_shape)
    return (query_arr, key_arr)


def draw_queries(key, part):
    return paired_draw(key)[0].astype(jnp.bfloat16)


def draw_keys(key, part):
    return paired_draw(key)[1].astype(jnp.bfloat16)


def draw_values(key, part):
    arr_shape = (TOKENS, H * DH)
    key_arr = paired_draw(key)[1]
    key_lift = lifted_draw(key_arr).reshape(TOKENS, H, DH)
    mixture = jnp.zeros((TOKENS, H, DH), jnp.float32)
    for term_index in range(3):
        column_order = jax.random.permutation(jax.random.fold_in(key, 30 + term_index), DH)
        magnitude = jax.random.uniform(jax.random.fold_in(key, 40 + term_index), (H, DH), jnp.float32, 0.4, 0.8)
        sign_draw = jax.random.uniform(jax.random.fold_in(key, 50 + term_index), (H, DH), jnp.float32)
        signed_coef = jnp.where(sign_draw < 0.5, -magnitude, magnitude)
        mixture = mixture + key_lift[:, :, column_order] * signed_coef[None]
    noise_key = jax.random.fold_in(key, 21)
    offset_key = jax.random.fold_in(key, 22)
    offsets = 0.7 * jnp.clip(jax.random.normal(offset_key, (TOKENS // SEG, 1, H * DH), jnp.float32), -3.0, 3.0)
    noise = jnp.clip(jax.random.normal(noise_key, arr_shape, jnp.float32), -3.0, 3.0)
    spread = jnp.broadcast_to(offsets, (TOKENS // SEG, SEG, H * DH)).reshape(arr_shape)
    total = mixture.reshape(arr_shape) + noise + spread
    return jnp.clip(total, -8.0, 8.0).astype(jnp.bfloat16)


def level_of(own_key, shape, pieces, least, largest):
    level, own = 1.0, jax.random.fold_in(own_key, 6)
    for axis_at, parts in pieces:
        steps = jnp.exp(jax.random.uniform(jax.random.fold_in(own, axis_at), (parts,), jnp.float32, least / len(pieces), largest / len(pieces)))
        level = level * jnp.repeat(steps, shape[axis_at] // parts).reshape([-1 if axis == axis_at else 1 for axis in range(len(shape))])
    return level


def bell_draw(key, dims, width, limit, pieces=(), kind=jnp.bfloat16):
    gain = level_of(key, dims, pieces, -0.22, 0.18) if pieces else 1.0
    entries = jax.random.normal(key, dims, jnp.float32) * width * gain
    return jnp.minimum(jnp.maximum(entries, -limit), limit).astype(kind)


def setup_inputs(seed: int = 0) -> dict:
    key_of = jax.random.split(jax.random.key(seed), 6)
    queries = draw_queries(jax.random.fold_in(key_of[5], 71), 0)
    keys = draw_keys(jax.random.fold_in(key_of[5], 71), 0)
    values = draw_values(jax.random.fold_in(key_of[5], 71), 0)
    gate_bias = jnp.clip(jax.random.uniform(key_of[3], (H,), jnp.float32, -3.0, 3.0) * level_of(key_of[3], (H,), ((0, 2),), -0.4, 0.0), -3.0, 3.0)
    out_weight = bell_draw(key_of[4], (H * DH, D), (H * DH) ** -0.5, 0.09375, ((0, 2),))
    return dict(queries=queries, keys=keys, values=values, gate_bias=gate_bias, out_weight=out_weight)


def lifted(source):
    return jnp.where(source > 0, source + 1.0, jnp.exp(jnp.minimum(source, 0.0)))

def reference(queries, keys, values, gate_bias, out_weight):
    seg_total = TOKENS // SEG
    query_blocks = queries.reshape(seg_total, SEG, H, DH)
    key_blocks = keys.reshape(seg_total, SEG, H, DH)
    value_blocks = values.reshape(seg_total, SEG, H, DH)
    mix_gate = jax.nn.sigmoid(gate_bias.astype(jnp.float32))[None, :, None]
    causal = jnp.arange(SEG)[:, None] >= jnp.arange(SEG)[None, :]

    def one_segment(running, blocks):
        memory, normalizer = running
        query_seg, key_seg, value_seg = blocks
        lift_query = lifted(query_seg.astype(jnp.float32)).astype(jnp.bfloat16)
        lift_key = lifted(key_seg.astype(jnp.float32)).astype(jnp.bfloat16)
        memory_b = memory.astype(jnp.bfloat16)
        numerator = jnp.einsum('qhd,hde->qhe', lift_query.astype(jnp.float32), memory_b.astype(jnp.float32))
        denominator = jnp.einsum('qhd,hd->qh', lift_query.astype(jnp.float32), normalizer, precision=lax.Precision.HIGHEST)
        mem_read = numerator / jnp.maximum(denominator, 1.0)[..., None]
        scores = jnp.einsum('qhd,khd->hqk', query_seg.astype(jnp.float32), key_seg.astype(jnp.float32)) / jnp.sqrt(jnp.float32(DH))
        scores = jnp.where(causal[None], scores, -jnp.inf)
        top_score = lax.optimization_barrier(jnp.max(scores, axis=-1, keepdims=True))
        expo = jnp.exp(scores - top_score)
        weights = (expo / lax.optimization_barrier(jnp.sum(expo, axis=-1, keepdims=True))).astype(jnp.bfloat16)
        local_part = jnp.einsum('hqk,khd->qhd', weights.astype(jnp.float32), value_seg.astype(jnp.float32))
        attn = (mix_gate * mem_read + (1.0 - mix_gate) * local_part).astype(jnp.bfloat16)
        mixed_seg = jnp.dot(attn.reshape(SEG, H * DH), out_weight, preferred_element_type=jnp.float32).astype(jnp.bfloat16)
        memory = memory + jnp.einsum('qhd,qhe->hde', lift_key.astype(jnp.float32), value_seg.astype(jnp.float32))
        normalizer = normalizer + lax.optimization_barrier(jnp.sum(lift_key.astype(jnp.float32), axis=0))
        return ((memory, normalizer), mixed_seg)
    start_state = (jnp.zeros((H, DH, DH), jnp.float32), jnp.zeros((H, DH), jnp.float32))
    final_state, mixed = lax.scan(one_segment, start_state, (query_blocks, key_blocks, value_blocks))
    return mixed.reshape(TOKENS, D)
```

```python
import functools

import jax
import jax.numpy as jnp
from jax import lax
from jax.experimental import pallas as pl
from jax.experimental.pallas import tpu as pltpu
from jax.sharding import PartitionSpec as P

SEG = 512
MESH = pl.DeviceIdType.MESH
F32 = jnp.float32
BF16 = jnp.bfloat16


def lifted(source):
    return jnp.where(source > 0, source + 1.0, jnp.exp(jnp.minimum(source, 0.0)))


def dot(a, b, dims):
    return lax.dot_general(a, b, ((dims[:1], dims[1:]), ((), ())), preferred_element_type=F32)


class Line:
    def __init__(self, size, place, device, refs):
        self.size, self.place, self.device = size, place, device
        if size == 2:
            self.inbox, self.send, self.recv = refs
        else:
            (self.right_in, self.left_in, self.right_out, self.left_out,
             self.right_send, self.right_recv, self.left_send, self.left_recv) = refs

    def swap(self, src, h):
        return pltpu.make_async_remote_copy(
            src.at[h], self.inbox.at[h], self.send.at[h], self.recv.at[h],
            device_id=self.device(1 - self.place), device_id_type=MESH)

    def to_right(self, src, h):
        return pltpu.make_async_remote_copy(
            src.at[h], self.right_in.at[h], self.right_send.at[h], self.right_recv.at[h],
            device_id=self.device(jnp.minimum(self.place + 1, self.size - 1)), device_id_type=MESH)

    def to_left(self, src, h):
        return pltpu.make_async_remote_copy(
            src.at[h], self.left_in.at[h], self.left_send.at[h], self.left_recv.at[h],
            device_id=self.device(jnp.maximum(self.place - 1, 0)), device_id_type=MESH)

    def begin(self, src, h):
        if self.size == 2:
            self.swap(src, h).start()
            return

        @pl.when(self.place == 0)
        def _():
            self.to_right(src, h).start()

        @pl.when(self.place == self.size - 1)
        def _():
            self.to_left(src, h).start()

    def finish(self, src, before, total, h, add):
        if self.size == 2:
            self.swap(src, h).wait_recv()
            got = self.inbox[h]
            total[h] = src[h] + got
            earlier = jnp.where(self.place > 0, got, jnp.zeros_like(got))
            before[h] = before[h] + earlier if add else earlier
            return
        place, last = self.place, self.size - 1
        total[h] = src[h]
        if not add:
            before[h] = jnp.zeros(before.shape[1:], F32)

        @pl.when(place > 0)
        def _():
            self.to_right(src, h).wait_recv()
            got = self.right_in[h]
            before[h] = before[h] + got
            total[h] = total[h] + got

            @pl.when(place < last)
            def _():
                self.right_out[h] = got + src[h]
                self.to_right(self.right_out, h).start()

        @pl.when(place < last)
        def _():
            self.to_left(src, h).wait_recv()
            got = self.left_in[h]
            total[h] = total[h] + got

            @pl.when(place > 0)
            def _():
                self.left_out[h] = got + src[h]
                self.to_left(self.left_out, h).start()

    def drain(self, src, h):
        if self.size == 2:
            self.swap(src, h).wait_send()
            return

        @pl.when(self.place < self.size - 1)
        def _():
            self.to_right(src, h).wait_send()

        @pl.when(self.place > 0)
        def _():
            self.to_left(src, h).wait_send()


def line_scratch(size, heads, state):
    box = pltpu.VMEM((heads,) + state, F32)
    sem = pltpu.SemaphoreType.DMA((heads,))
    return [box, sem, sem] if size == 2 else [box] * 4 + [sem] * 4


GROUP = 4


def kernel(sizes, tile, gate, q_hbm, k_hbm, v_hbm, w_hbm, o_hbm, *scratch):
    x_size, y_size, z_size = sizes
    scratch = list(scratch)

    def take(count):
        taken = scratch[:count]
        del scratch[:count]
        return taken

    qb, kb, vb, wb, loc, attn, acc, peer, outb = take(9)
    own, row_sum, plane_sum, before, z_in = take(5)
    q_sem, k_sem, v_sem, w_sem, o_sem = take(5)
    z_send, z_recv, peer_send, peer_recv = take(4)
    x_refs = take(3 if x_size == 2 else 8)
    y_refs = take(3 if y_size == 2 else 8)

    heads, rows, width = qb.shape
    half = rows // 2
    tiles = acc.shape[0]
    depth = GROUP * width
    groups = heads // GROUP
    seq, core = lax.axis_index("seq"), lax.axis_index("head")
    x = lax.rem(seq, x_size)
    y = lax.rem(seq // x_size, y_size)
    z = seq // (x_size * y_size)

    def at(xx, yy, zz):
        return ((zz * y_size + yy) * x_size + xx, core)

    x_line = Line(x_size, x, lambda c: at(c, y, z), x_refs)
    y_line = Line(y_size, y, lambda c: at(x, c, z), y_refs)
    other = 1 - core

    def load(src, dst, sem, h):
        return pltpu.make_async_copy(
            src.at[:, pl.ds(pl.multiple_of(h * width, width), width)], dst.at[h], sem.at[h])

    def load_w(g):
        part = pl.ds(pl.multiple_of(g * depth, depth), depth)
        return pltpu.make_async_copy(w_hbm.at[part, :], wb.at[part, :], w_sem.at[g])

    def start_loads(h, _):
        load(k_hbm, kb, k_sem, h).start()
        load(v_hbm, vb, v_sem, h).start()
        return 0

    def start_queries(h, _):
        load(q_hbm, qb, q_sem, h).start()
        return 0

    def start_weights(g, _):
        load_w(g).start()
        return 0

    lax.fori_loop(0, heads, start_loads, 0)
    lax.fori_loop(0, heads, start_queries, 0)
    lax.fori_loop(0, groups, start_weights, 0)

    barrier = pltpu.get_barrier_semaphore()
    pl.semaphore_signal(barrier, inc=1, device_id=(seq, other), device_id_type=MESH)
    greeted = 1
    for place, size, where in (
        (x, x_size, lambda c: at(c, y, z)),
        (y, y_size, lambda c: at(x, c, z)),
        (z, z_size, lambda c: at(x, y, c)),
    ):
        @pl.when(place > 0)
        def _():
            pl.semaphore_signal(barrier, inc=1, device_id=where(place - 1), device_id_type=MESH)

        @pl.when(place < size - 1)
        def _():
            pl.semaphore_signal(barrier, inc=1, device_id=where(place + 1), device_id_type=MESH)

        greeted = greeted + (place > 0).astype(jnp.int32) + (place < size - 1).astype(jnp.int32)
    pl.semaphore_wait(barrier, greeted)

    def z_copy(src, h):
        return pltpu.make_async_remote_copy(
            src.at[h], z_in.at[h], z_send.at[h], z_recv.at[h],
            device_id=at(x, y, jnp.minimum(z + 1, z_size - 1)), device_id_type=MESH)

    def update(h):
        load(k_hbm, kb, k_sem, h).wait()
        load(v_hbm, vb, v_sem, h).wait()
        lift_key = lifted(kb[h].astype(F32)).astype(BF16)
        own[h, pl.ds(0, width), :] = dot(lift_key, vb[h], (0, 0))
        zsum = jnp.sum(lift_key.astype(F32), axis=0, keepdims=True)
        own[h, pl.ds(width, 8), :] = jnp.broadcast_to(zsum, (8, width))
        x_line.begin(own, h)

    def local(h):
        load(q_hbm, qb, q_sem, h).wait()
        rate = 1.4426950408889634 / (width ** 0.5)
        keep = 1.0 / (1.0 + jnp.exp(jnp.full((1, width), gate[h], F32)))
        causal = (lax.broadcasted_iota(jnp.int32, (half, half), 0)
                  >= lax.broadcasted_iota(jnp.int32, (half, half), 1))
        for part in range(2):
            rows_here = pl.ds(part * half, half)
            qs = qb[h, rows_here, :]
            diag = jnp.where(causal, dot(qs, kb[h, rows_here, :], (1, 1)), -jnp.inf)
            top = jnp.max(diag, axis=-1, keepdims=True)
            if part == 1:
                past = dot(qs, kb[h, pl.ds(0, half), :], (1, 1))
                top = jnp.maximum(top, jnp.max(past, axis=-1, keepdims=True))
                past = jnp.exp2((past - top) * rate)
            diag = jnp.exp2((diag - top) * rate)
            total = jnp.sum(diag, axis=-1, keepdims=True)
            if part == 1:
                total = total + jnp.sum(past, axis=-1, keepdims=True)
            inverse = 1.0 / total
            out = dot((diag * inverse).astype(BF16), vb[h, rows_here, :], (1, 0))
            if part == 1:
                out = out + dot((past * inverse).astype(BF16), vb[h, pl.ds(0, half), :], (1, 0))
            loc[h, rows_here, :] = out * keep

    def z_stage(h):
        @pl.when(z > 0)
        def _():
            z_copy(plane_sum, h).wait_recv()
            got = z_in[h]
            before[h] = before[h] + got
            plane_sum[h] = plane_sum[h] + got

        @pl.when(z < z_size - 1)
        def _():
            z_copy(plane_sum, h).start()

    def read(h):
        share = 1.0 / (1.0 + jnp.exp(jnp.full((1, width), -gate[h], F32)))
        lift_query = lifted(qb[h].astype(F32)).astype(BF16)
        memory = before[h, pl.ds(0, width), :].astype(BF16)
        numerator = dot(lift_query, memory, (1, 0))
        norm = before[h, pl.ds(width, 1), :]
        denominator = jnp.sum(lift_query.astype(F32) * norm, axis=-1, keepdims=True)
        inverse = 1.0 / jnp.maximum(denominator, 1.0)
        value = numerator * inverse * share + loc[h]
        attn[:, pl.ds(pl.multiple_of(h * width, width), width)] = value.astype(BF16)

    def columns(n):
        return pl.ds(pl.multiple_of(n * tile, tile), tile)

    def project(g):
        load_w(g).wait()
        part = pl.ds(pl.multiple_of(g * depth, depth), depth)

        def one(n, _):
            product = dot(attn[:, part], wb[part, columns(n)], (1, 0))

            @pl.when(g == 0)
            def _():
                acc[n] = product

            @pl.when(g > 0)
            def _():
                acc[n] = acc[n] + product
            return 0

        lax.fori_loop(0, tiles, one, 0)

    x_lag, y_lag = 1, 2
    z_lag = y_lag + 2 * z

    def within(h):
        return jnp.logical_and(h >= 0, h < heads)

    def step(i, _):
        @pl.when(2 * i < heads)
        def _():
            update(2 * i)
            update(2 * i + 1)

        @pl.when(within(i - x_lag))
        def _():
            h = i - x_lag
            x_line.finish(own, before, row_sum, h, False)
            y_line.begin(row_sum, h)

        @pl.when(within(i - y_lag))
        def _():
            y_line.finish(row_sum, before, plane_sum, i - y_lag, True)

        @pl.when(within(i - z_lag))
        def _():
            z_stage(i - z_lag)

        @pl.when(i < heads)
        def _():
            local(i)

        @pl.when(within(i - z_lag))
        def _():
            h = i - z_lag
            read(h)

            @pl.when(jnp.logical_and(lax.rem(h, GROUP) == GROUP - 1, h < heads - 1))
            def _():
                project(h // GROUP)
        return 0

    lax.fori_loop(0, heads + y_lag + 2 * (z_size - 1), step, 0)

    last = pl.ds((groups - 1) * depth, depth)
    load_w(groups - 1).wait()
    theirs = pl.ds(pl.multiple_of(other * half, half), half)
    mine = pl.ds(pl.multiple_of(core * half, half), half)

    def to_peer(n):
        return pltpu.make_async_remote_copy(
            acc.at[n, theirs, :], peer.at[n], peer_send.at[n], peer_recv.at[n],
            device_id=(seq, other), device_id_type=MESH)

    def result(n):
        return pltpu.make_async_copy(outb.at[:, columns(n)], o_hbm.at[:, columns(n)], o_sem.at[n])

    def send_tile(n, _):
        acc[n, theirs, :] = acc[n, theirs, :] + dot(attn[theirs, last], wb[last, columns(n)], (1, 0))
        to_peer(n).start()
        return 0

    def own_tile(n, _):
        value = acc[n, mine, :] + dot(attn[mine, last], wb[last, columns(n)], (1, 0))
        to_peer(n).wait_recv()
        outb[:, columns(n)] = (value + peer[n]).astype(BF16)
        result(n).start()
        return 0

    lax.fori_loop(0, tiles, send_tile, 0)
    lax.fori_loop(0, tiles, own_tile, 0)

    def drain(h, _):
        x_line.drain(own, h)
        y_line.drain(row_sum, h)

        @pl.when(z < z_size - 1)
        def _():
            z_copy(plane_sum, h).wait_send()
        return 0

    def drain_tiles(n, _):
        to_peer(n).wait_send()
        result(n).wait()
        return 0

    lax.fori_loop(0, heads, drain, 0)
    lax.fori_loop(0, tiles, drain_tiles, 0)


def on_device(sizes, queries, keys, values, gate_bias, out_weight):
    heads = gate_bias.shape[0]
    rows, feat = queries.shape
    width = feat // heads
    model = out_weight.shape[1]
    tile = 512
    tiles = model // tile
    state = (width + 8, width)
    box = pltpu.VMEM((heads,) + state, F32)
    sem = pltpu.SemaphoreType.DMA((heads,))
    tile_sem = pltpu.SemaphoreType.DMA((tiles,))
    blocks = pltpu.VMEM((heads, rows, width), BF16)
    scratch = [
        blocks, blocks, blocks,
        pltpu.VMEM(out_weight.shape, BF16),
        pltpu.VMEM((heads, rows, width), F32),
        pltpu.VMEM((rows, feat), BF16),
        pltpu.VMEM((tiles, rows, tile), F32),
        pltpu.VMEM((tiles, rows // 2, tile), F32),
        pltpu.VMEM((rows // 2, model), BF16),
        box, box, box, box, box,
        sem, sem, sem, pltpu.SemaphoreType.DMA((heads // GROUP,)), tile_sem,
        sem, sem, tile_sem, tile_sem,
    ] + line_scratch(sizes[0], heads, state) + line_scratch(sizes[1], heads, state)
    hbm = pl.BlockSpec(memory_space=pl.ANY)
    return pl.pallas_call(
        functools.partial(kernel, sizes, tile),
        out_shape=jax.ShapeDtypeStruct((rows // 2, model), BF16),
        in_specs=[pl.BlockSpec(memory_space=pltpu.SMEM), hbm, hbm, hbm, hbm],
        out_specs=hbm,
        scratch_shapes=scratch,
        compiler_params=pltpu.CompilerParams(
            collective_id=0, has_side_effects=True, vmem_limit_bytes=62 * 1024 * 1024),
        cost_estimate=pl.CostEstimate(
            flops=2 * rows * feat * (model + rows + 2 * width), bytes_accessed=24 * 1024 * 1024,
            transcendentals=heads * rows * rows),
    )(gate_bias, queries, keys, values, out_weight)


def grid_of(count):
    z_size = min(4, count)
    plane = count // z_size
    y_size = 1
    while y_size * y_size < plane:
        y_size *= 2
    return (plane // y_size, y_size, z_size)


def solution(mesh):
    in_specs = (P("seq", "head"), P("seq", "head"), P("seq", "head"), P("head"), P("head", None))
    out_specs = P(("seq", "head"), None)
    return jax.shard_map(
        functools.partial(on_device, grid_of(mesh.shape["seq"])),
        mesh=mesh, in_specs=in_specs, out_specs=out_specs, check_vma=False
    )
```

```python
import functools

import jax
import jax.numpy as jnp
from jax import lax
from jax.experimental import pallas as pl
from jax.experimental.pallas import tpu as pltpu
from jax.sharding import PartitionSpec as P

SEG = 512
MESH = pl.DeviceIdType.MESH
F32 = jnp.float32
BF16 = jnp.bfloat16


def lifted(source):
    return jnp.where(source > 0, source + 1.0, jnp.exp(jnp.minimum(source, 0.0)))


def dot(a, b, dims):
    return lax.dot_general(a, b, ((dims[:1], dims[1:]), ((), ())), preferred_element_type=F32)


class Line:
    def __init__(self, size, place, device, refs):
        self.size, self.place, self.device = size, place, device
        if size == 2:
            self.inbox, self.send, self.recv = refs
        else:
            (self.right_in, self.left_in, self.right_out, self.left_out,
             self.right_send, self.right_recv, self.left_send, self.left_recv) = refs

    def swap(self, src, h):
        return pltpu.make_async_remote_copy(
            src.at[h], self.inbox.at[h], self.send.at[h], self.recv.at[h],
            device_id=self.device(1 - self.place), device_id_type=MESH)

    def to_right(self, src, h):
        return pltpu.make_async_remote_copy(
            src.at[h], self.right_in.at[h], self.right_send.at[h], self.right_recv.at[h],
            device_id=self.device(jnp.minimum(self.place + 1, self.size - 1)), device_id_type=MESH)

    def to_left(self, src, h):
        return pltpu.make_async_remote_copy(
            src.at[h], self.left_in.at[h], self.left_send.at[h], self.left_recv.at[h],
            device_id=self.device(jnp.maximum(self.place - 1, 0)), device_id_type=MESH)

    def begin(self, src, h):
        if self.size == 2:
            self.swap(src, h).start()
            return

        @pl.when(self.place == 0)
        def _():
            self.to_right(src, h).start()

        @pl.when(self.place == self.size - 1)
        def _():
            self.to_left(src, h).start()

    def finish(self, src, before, total, h, add):
        if self.size == 2:
            self.swap(src, h).wait_recv()
            got = self.inbox[h]
            total[h] = src[h] + got
            earlier = jnp.where(self.place > 0, got, jnp.zeros_like(got))
            before[h] = before[h] + earlier if add else earlier
            return
        place, last = self.place, self.size - 1
        total[h] = src[h]
        if not add:
            before[h] = jnp.zeros(before.shape[1:], F32)

        @pl.when(place > 0)
        def _():
            self.to_right(src, h).wait_recv()
            got = self.right_in[h]
            before[h] = before[h] + got
            total[h] = total[h] + got

            @pl.when(place < last)
            def _():
                self.right_out[h] = got + src[h]
                self.to_right(self.right_out, h).start()

        @pl.when(place < last)
        def _():
            self.to_left(src, h).wait_recv()
            got = self.left_in[h]
            total[h] = total[h] + got

            @pl.when(place > 0)
            def _():
                self.left_out[h] = got + src[h]
                self.to_left(self.left_out, h).start()

    def drain(self, src, h):
        if self.size == 2:
            self.swap(src, h).wait_send()
            return

        @pl.when(self.place < self.size - 1)
        def _():
            self.to_right(src, h).wait_send()

        @pl.when(self.place > 0)
        def _():
            self.to_left(src, h).wait_send()


def line_scratch(size, heads, state):
    box = pltpu.VMEM((heads,) + state, F32)
    sem = pltpu.SemaphoreType.DMA((heads,))
    return [box, sem, sem] if size == 2 else [box] * 4 + [sem] * 4


GROUP = 8


def kernel(sizes, tile, gate, q_hbm, k_hbm, v_hbm, w_hbm, o_hbm, *scratch):
    x_size, y_size, z_size = sizes
    scratch = list(scratch)

    def take(count):
        taken = scratch[:count]
        del scratch[:count]
        return taken

    qb, kb, vb, wb, loc, attn, acc, peer, outb = take(9)
    own, row_sum, plane_sum, before, z_in = take(5)
    q_sem, k_sem, v_sem, w_sem, o_sem = take(5)
    z_send, z_recv, peer_send, peer_recv = take(4)
    x_refs = take(3 if x_size == 2 else 8)
    y_refs = take(3 if y_size == 2 else 8)

    heads, rows, width = qb.shape
    half = rows // 2
    tiles = acc.shape[0]
    depth = GROUP * width
    groups = heads // GROUP
    seq, core = lax.axis_index("seq"), lax.axis_index("head")
    x = lax.rem(seq, x_size)
    y = lax.rem(seq // x_size, y_size)
    z = seq // (x_size * y_size)

    def at(xx, yy, zz):
        return ((zz * y_size + yy) * x_size + xx, core)

    x_line = Line(x_size, x, lambda c: at(c, y, z), x_refs)
    y_line = Line(y_size, y, lambda c: at(x, c, z), y_refs)
    other = 1 - core

    def load(src, dst, sem, h):
        return pltpu.make_async_copy(
            src.at[:, pl.ds(pl.multiple_of(h * width, width), width)], dst.at[h], sem.at[h])

    def load_w(g):
        part = pl.ds(pl.multiple_of(g * depth, depth), depth)
        return pltpu.make_async_copy(w_hbm.at[part, :], wb.at[part, :], w_sem.at[g])

    def start_loads(h, _):
        load(k_hbm, kb, k_sem, h).start()
        load(v_hbm, vb, v_sem, h).start()
        return 0

    def start_queries(h, _):
        load(q_hbm, qb, q_sem, h).start()
        return 0

    def start_weights(g, _):
        load_w(g).start()
        return 0

    lax.fori_loop(0, heads, start_loads, 0)
    lax.fori_loop(0, heads, start_queries, 0)
    lax.fori_loop(0, groups, start_weights, 0)

    barrier = pltpu.get_barrier_semaphore()
    pl.semaphore_signal(barrier, inc=1, device_id=(seq, other), device_id_type=MESH)
    greeted = 1
    for place, size, where in (
        (x, x_size, lambda c: at(c, y, z)),
        (y, y_size, lambda c: at(x, c, z)),
        (z, z_size, lambda c: at(x, y, c)),
    ):
        @pl.when(place > 0)
        def _():
            pl.semaphore_signal(barrier, inc=1, device_id=where(place - 1), device_id_type=MESH)

        @pl.when(place < size - 1)
        def _():
            pl.semaphore_signal(barrier, inc=1, device_id=where(place + 1), device_id_type=MESH)

        greeted = greeted + (place > 0).astype(jnp.int32) + (place < size - 1).astype(jnp.int32)
    pl.semaphore_wait(barrier, greeted)

    def z_copy(src, h):
        return pltpu.make_async_remote_copy(
            src.at[h], z_in.at[h], z_send.at[h], z_recv.at[h],
            device_id=at(x, y, jnp.minimum(z + 1, z_size - 1)), device_id_type=MESH)

    def update(h):
        lift_key = lifted(kb[h].astype(F32)).astype(BF16)
        own[h, pl.ds(0, width), :] = dot(lift_key, vb[h], (0, 0))
        zsum = jnp.sum(lift_key.astype(F32), axis=0, keepdims=True)
        own[h, pl.ds(width, 8), :] = jnp.broadcast_to(zsum, (8, width))

    def local(h):
        rate = 1.4426950408889634 / (width ** 0.5)
        keep = 1.0 / (1.0 + jnp.exp(jnp.full((1, width), gate[h], F32)))
        causal = (lax.broadcasted_iota(jnp.int32, (half, half), 0)
                  >= lax.broadcasted_iota(jnp.int32, (half, half), 1))
        for part in range(2):
            rows_here = pl.ds(part * half, half)
            qs = qb[h, rows_here, :]
            diag = jnp.where(causal, dot(qs, kb[h, rows_here, :], (1, 1)), -jnp.inf)
            top = jnp.max(diag, axis=-1, keepdims=True)
            if part == 1:
                past = dot(qs, kb[h, pl.ds(0, half), :], (1, 1))
                top = jnp.maximum(top, jnp.max(past, axis=-1, keepdims=True))
                past = jnp.exp2((past - top) * rate)
            diag = jnp.exp2((diag - top) * rate)
            total = jnp.sum(diag, axis=-1, keepdims=True)
            if part == 1:
                total = total + jnp.sum(past, axis=-1, keepdims=True)
            inverse = 1.0 / total
            out = dot((diag * inverse).astype(BF16), vb[h, rows_here, :], (1, 0))
            if part == 1:
                out = out + dot((past * inverse).astype(BF16), vb[h, pl.ds(0, half), :], (1, 0))
            loc[h, rows_here, :] = out * keep

    def z_stage(h):
        @pl.when(z > 0)
        def _():
            z_copy(plane_sum, h).wait_recv()
            got = z_in[h]
            before[h] = before[h] + got

            @pl.when(z < z_size - 1)
            def _():
                plane_sum[h] = plane_sum[h] + got
                z_copy(plane_sum, h).start()

    def read(h):
        share = 1.0 / (1.0 + jnp.exp(jnp.full((1, width), -gate[h], F32)))
        lift_query = lifted(qb[h].astype(F32)).astype(BF16)
        memory = before[h, pl.ds(0, width), :].astype(BF16)
        numerator = dot(lift_query, memory, (1, 0))
        norm = before[h, pl.ds(width, 1), :]
        denominator = jnp.sum(lift_query.astype(F32) * norm, axis=-1, keepdims=True)
        inverse = 1.0 / jnp.maximum(denominator, 1.0)
        value = numerator * inverse * share + loc[h]
        attn[:, pl.ds(pl.multiple_of(h * width, width), width)] = value.astype(BF16)

    def columns(n):
        return pl.ds(pl.multiple_of(n * tile, tile), tile)

    def project_first():
        load_w(0).wait()
        part = pl.ds(0, depth)

        def one(n, _):
            acc[n] = dot(attn[:, part], wb[part, columns(n)], (1, 0))
            return 0

        lax.fori_loop(0, tiles, one, 0)

    pairs = heads // 2

    def update_pair(j, _):
        pair = (2 * j, 2 * j + 1)
        for h in pair:
            load(k_hbm, kb, k_sem, h).wait()
            load(v_hbm, vb, v_sem, h).wait()
        for h in pair:
            update(h)
        for h in pair:
            x_line.begin(own, h)
        return 0

    lax.fori_loop(0, pairs, update_pair, 0)

    def within(j):
        return jnp.logical_and(j >= 0, j < pairs)

    def step(i, _):
        @pl.when(i < pairs)
        def _():
            pair = (2 * i, 2 * i + 1)
            for h in pair:
                x_line.finish(own, before, row_sum, h, False)
                y_line.begin(row_sum, h)
            for h in pair:
                load(q_hbm, qb, q_sem, h).wait()
            for h in pair:
                local(h)

        @pl.when(within(i - 1))
        def _():
            for h in (2 * i - 2, 2 * i - 1):
                y_line.finish(row_sum, before, plane_sum, h, True)

                @pl.when(z == 0)
                def _():
                    z_copy(plane_sum, h).start()

        @pl.when(within(i - 1 - z))
        def _():
            j = i - 1 - z
            pair = (2 * j, 2 * j + 1)
            for h in pair:
                z_stage(h)
            for h in pair:
                read(h)

            @pl.when(j == GROUP // 2 - 1)
            def _():
                project_first()
        return 0

    lax.fori_loop(0, pairs + z_size, step, 0)

    last = pl.ds((groups - 1) * depth, depth)
    load_w(groups - 1).wait()
    theirs = pl.ds(pl.multiple_of(other * half, half), half)
    mine = pl.ds(pl.multiple_of(core * half, half), half)

    def to_peer(n):
        return pltpu.make_async_remote_copy(
            acc.at[n, theirs, :], peer.at[n], peer_send.at[n], peer_recv.at[n],
            device_id=(seq, other), device_id_type=MESH)

    def result(n):
        return pltpu.make_async_copy(outb.at[:, columns(n)], o_hbm.at[:, columns(n)], o_sem.at[n])

    def send_tile(n, _):
        acc[n, theirs, :] = acc[n, theirs, :] + dot(attn[theirs, last], wb[last, columns(n)], (1, 0))
        to_peer(n).start()
        return 0

    def own_tile(n, _):
        value = acc[n, mine, :] + dot(attn[mine, last], wb[last, columns(n)], (1, 0))
        to_peer(n).wait_recv()
        outb[:, columns(n)] = (value + peer[n]).astype(BF16)
        result(n).start()
        return 0

    lax.fori_loop(0, tiles, send_tile, 0)
    lax.fori_loop(0, tiles, own_tile, 0)

    def drain(h, _):
        x_line.drain(own, h)
        y_line.drain(row_sum, h)

        @pl.when(z < z_size - 1)
        def _():
            z_copy(plane_sum, h).wait_send()
        return 0

    def drain_tiles(n, _):
        to_peer(n).wait_send()
        result(n).wait()
        return 0

    lax.fori_loop(0, heads, drain, 0)
    lax.fori_loop(0, tiles, drain_tiles, 0)


def on_device(sizes, queries, keys, values, gate_bias, out_weight):
    heads = gate_bias.shape[0]
    rows, feat = queries.shape
    width = feat // heads
    model = out_weight.shape[1]
    tile = 512
    tiles = model // tile
    state = (width + 8, width)
    box = pltpu.VMEM((heads,) + state, F32)
    sem = pltpu.SemaphoreType.DMA((heads,))
    tile_sem = pltpu.SemaphoreType.DMA((tiles,))
    blocks = pltpu.VMEM((heads, rows, width), BF16)
    scratch = [
        blocks, blocks, blocks,
        pltpu.VMEM(out_weight.shape, BF16),
        pltpu.VMEM((heads, rows, width), F32),
        pltpu.VMEM((rows, feat), BF16),
        pltpu.VMEM((tiles, rows, tile), F32),
        pltpu.VMEM((tiles, rows // 2, tile), F32),
        pltpu.VMEM((rows // 2, model), BF16),
        box, box, box, box, box,
        sem, sem, sem, pltpu.SemaphoreType.DMA((heads // GROUP,)), tile_sem,
        sem, sem, tile_sem, tile_sem,
    ] + line_scratch(sizes[0], heads, state) + line_scratch(sizes[1], heads, state)
    hbm = pl.BlockSpec(memory_space=pl.ANY)
    return pl.pallas_call(
        functools.partial(kernel, sizes, tile),
        out_shape=jax.ShapeDtypeStruct((rows // 2, model), BF16),
        in_specs=[pl.BlockSpec(memory_space=pltpu.SMEM), hbm, hbm, hbm, hbm],
        out_specs=hbm,
        scratch_shapes=scratch,
        compiler_params=pltpu.CompilerParams(
            collective_id=0, has_side_effects=True, vmem_limit_bytes=62 * 1024 * 1024),
        cost_estimate=pl.CostEstimate(
            flops=2 * rows * feat * (model + rows + 2 * width), bytes_accessed=24 * 1024 * 1024,
            transcendentals=heads * rows * rows),
    )(gate_bias, queries, keys, values, out_weight)


def grid_of(count):
    z_size = min(4, count)
    plane = count // z_size
    y_size = 1
    while y_size * y_size < plane:
        y_size *= 2
    return (plane // y_size, y_size, z_size)


def solution(mesh):
    in_specs = (P("seq", "head"), P("seq", "head"), P("seq", "head"), P("head"), P("head", None))
    out_specs = P(("seq", "head"), None)
    return jax.shard_map(
        functools.partial(on_device, grid_of(mesh.shape["seq"])),
        mesh=mesh, in_specs=in_specs, out_specs=out_specs, check_vma=False
    )
```

```python
import functools

import jax
import jax.numpy as jnp
from jax import lax
from jax.experimental import pallas as pl
from jax.experimental.pallas import tpu as pltpu
from jax.sharding import PartitionSpec as P

SEG = 512
MESH = pl.DeviceIdType.MESH
F32 = jnp.float32
BF16 = jnp.bfloat16


def lifted(source):
    return jnp.where(source > 0, source + 1.0, jnp.exp(jnp.minimum(source, 0.0)))


def dot(a, b, dims):
    return lax.dot_general(a, b, ((dims[:1], dims[1:]), ((), ())), preferred_element_type=F32)


class Line:
    def __init__(self, size, place, device, refs):
        self.size, self.place, self.device = size, place, device
        if size == 2:
            self.inbox, self.send, self.recv = refs
        else:
            (self.right_in, self.left_in, self.right_out, self.left_out,
             self.right_send, self.right_recv, self.left_send, self.left_recv) = refs

    def swap(self, src, h):
        return pltpu.make_async_remote_copy(
            src.at[h], self.inbox.at[h], self.send.at[h], self.recv.at[h],
            device_id=self.device(1 - self.place), device_id_type=MESH)

    def to_right(self, src, h):
        return pltpu.make_async_remote_copy(
            src.at[h], self.right_in.at[h], self.right_send.at[h], self.right_recv.at[h],
            device_id=self.device(jnp.minimum(self.place + 1, self.size - 1)), device_id_type=MESH)

    def to_left(self, src, h):
        return pltpu.make_async_remote_copy(
            src.at[h], self.left_in.at[h], self.left_send.at[h], self.left_recv.at[h],
            device_id=self.device(jnp.maximum(self.place - 1, 0)), device_id_type=MESH)

    def begin(self, src, h):
        if self.size == 2:
            self.swap(src, h).start()
            return

        @pl.when(self.place == 0)
        def _():
            self.to_right(src, h).start()

        @pl.when(self.place == self.size - 1)
        def _():
            self.to_left(src, h).start()

    def finish(self, src, before, total, h, add):
        if self.size == 2:
            self.swap(src, h).wait_recv()
            got = self.inbox[h]
            total[h] = src[h] + got
            earlier = jnp.where(self.place > 0, got, jnp.zeros_like(got))
            before[h] = before[h] + earlier if add else earlier
            return
        place, last = self.place, self.size - 1
        total[h] = src[h]
        if not add:
            before[h] = jnp.zeros(before.shape[1:], F32)

        @pl.when(place > 0)
        def _():
            self.to_right(src, h).wait_recv()
            got = self.right_in[h]
            before[h] = before[h] + got
            total[h] = total[h] + got

            @pl.when(place < last)
            def _():
                self.right_out[h] = got + src[h]
                self.to_right(self.right_out, h).start()

        @pl.when(place < last)
        def _():
            self.to_left(src, h).wait_recv()
            got = self.left_in[h]
            total[h] = total[h] + got

            @pl.when(place > 0)
            def _():
                self.left_out[h] = got + src[h]
                self.to_left(self.left_out, h).start()

    def drain(self, src, h):
        if self.size == 2:
            self.swap(src, h).wait_send()
            return

        @pl.when(self.place < self.size - 1)
        def _():
            self.to_right(src, h).wait_send()

        @pl.when(self.place > 0)
        def _():
            self.to_left(src, h).wait_send()


def line_scratch(size, heads, state):
    box = pltpu.VMEM((heads,) + state, F32)
    sem = pltpu.SemaphoreType.DMA((heads,))
    return [box, sem, sem] if size == 2 else [box] * 4 + [sem] * 4


GROUP = 8
PAD = 16
LEAD = 2


def kernel(sizes, tile, gate, q_hbm, k_hbm, v_hbm, w_hbm, o_hbm, *scratch):
    x_size, y_size, z_size = sizes
    scratch = list(scratch)

    def take(count):
        taken = scratch[:count]
        del scratch[:count]
        return taken

    qb, kb, vb, vt, wb, loc, attn, acc, peer, outb = take(10)
    own, row_sum, plane_sum, before, z_in = take(5)
    q_sem, k_sem, v_sem, w_sem, o_sem = take(5)
    z_send, z_recv, peer_send, peer_recv = take(4)
    x_refs = take(3 if x_size == 2 else 8)
    y_refs = take(3 if y_size == 2 else 8)

    heads, rows, width = qb.shape
    half = rows // 2
    tiles = acc.shape[0]
    depth = GROUP * width
    groups = heads // GROUP
    seq, core = lax.axis_index("seq"), lax.axis_index("head")
    x = lax.rem(seq, x_size)
    y = lax.rem(seq // x_size, y_size)
    z = seq // (x_size * y_size)

    def at(xx, yy, zz):
        return ((zz * y_size + yy) * x_size + xx, core)

    x_line = Line(x_size, x, lambda c: at(c, y, z), x_refs)
    y_line = Line(y_size, y, lambda c: at(x, c, z), y_refs)
    other = 1 - core

    def load(src, dst, sem, h):
        return pltpu.make_async_copy(
            src.at[:, pl.ds(pl.multiple_of(h * width, width), width)], dst.at[h], sem.at[h])

    def load_w(g):
        part = pl.ds(pl.multiple_of(g * depth, depth), depth)
        return pltpu.make_async_copy(w_hbm.at[part, :], wb.at[part, :], w_sem.at[g])

    def start_loads(h, _):
        load(k_hbm, kb, k_sem, h).start()
        load(v_hbm, vb, v_sem, h).start()
        return 0

    def start_queries(h, _):
        load(q_hbm, qb, q_sem, h).start()
        return 0

    def start_weights(g, _):
        load_w(g).start()
        return 0

    lax.fori_loop(0, heads, start_loads, 0)
    lax.fori_loop(0, heads, start_queries, 0)
    lax.fori_loop(0, groups, start_weights, 0)

    barrier = pltpu.get_barrier_semaphore()
    pl.semaphore_signal(barrier, inc=1, device_id=(seq, other), device_id_type=MESH)
    greeted = 1
    for place, size, where in (
        (x, x_size, lambda c: at(c, y, z)),
        (y, y_size, lambda c: at(x, c, z)),
        (z, z_size, lambda c: at(x, y, c)),
    ):
        @pl.when(place > 0)
        def _():
            pl.semaphore_signal(barrier, inc=1, device_id=where(place - 1), device_id_type=MESH)

        @pl.when(place < size - 1)
        def _():
            pl.semaphore_signal(barrier, inc=1, device_id=where(place + 1), device_id_type=MESH)

        greeted = greeted + (place > 0).astype(jnp.int32) + (place < size - 1).astype(jnp.int32)
    pl.semaphore_wait(barrier, greeted)

    def z_copy(src, h):
        return pltpu.make_async_remote_copy(
            src.at[h], z_in.at[h], z_send.at[h], z_recv.at[h],
            device_id=at(x, y, jnp.minimum(z + 1, z_size - 1)), device_id_type=MESH)

    def update(h):
        lift_key = lifted(kb[h].astype(F32)).astype(BF16)
        vt[h, pl.ds(0, width), :] = vb[h].T
        vt[h, pl.ds(width, PAD), :] = jnp.ones((PAD, rows), BF16)
        own[h] = dot(vt[h], lift_key, (1, 0))[:width + 8]

    def local(h):
        rate = 1.4426950408889634 / (width ** 0.5)
        keep = 1.0 / (1.0 + jnp.exp(jnp.full((1, half), gate[h], F32)))
        causal = (lax.broadcasted_iota(jnp.int32, (half, half), 0)
                  <= lax.broadcasted_iota(jnp.int32, (half, half), 1))
        for part in range(2):
            here = pl.ds(part * half, half)
            qs = qb[h, here, :]
            diag = jnp.where(causal, dot(kb[h, here, :], qs, (1, 1)), -jnp.inf)
            top = jnp.max(diag, axis=0, keepdims=True)
            if part == 1:
                past = dot(kb[h, pl.ds(0, half), :], qs, (1, 1))
                top = jnp.maximum(top, jnp.max(past, axis=0, keepdims=True))
                past = jnp.exp2((past - top) * rate).astype(BF16)
            diag = jnp.exp2((diag - top) * rate).astype(BF16)
            out = dot(vt[h, :, here], diag, (1, 0))
            if part == 1:
                out = out + dot(vt[h, :, pl.ds(0, half)], past, (1, 0))
            loc[h, :, here] = out[:width] * (keep / out[width:width + 1])

    def z_stage(h):
        @pl.when(z > 0)
        def _():
            z_copy(plane_sum, h).wait_recv()
            got = z_in[h]
            before[h] = before[h] + got

            @pl.when(z < z_size - 1)
            def _():
                plane_sum[h] = plane_sum[h] + got
                z_copy(plane_sum, h).start()

    def read(h):
        share = 1.0 / (1.0 + jnp.exp(jnp.full((1, rows), -gate[h], F32)))
        lift_query = lifted(qb[h].astype(F32)).astype(BF16)
        norm = before[h, pl.ds(width, 1), :]
        high = norm.astype(BF16).astype(F32)
        middle = (norm - high).astype(BF16).astype(F32)
        low = norm - high - middle
        row = lax.broadcasted_iota(jnp.int32, (PAD, width), 0)
        parts = jnp.where(row == 0, high, jnp.where(row == 1, middle, jnp.where(row == 2, low, 0.0)))
        memory = before[h, pl.ds(0, width), :].astype(BF16)
        got = dot(jnp.concatenate([memory, parts.astype(BF16)], axis=0), lift_query, (1, 1))
        denominator = jnp.sum(got[width:width + 8], axis=0, keepdims=True)
        value = got[:width] * (share / jnp.maximum(denominator, 1.0)) + loc[h]
        attn[:, pl.ds(pl.multiple_of(h * width, width), width)] = value.astype(BF16).T

    def columns(n):
        return pl.ds(pl.multiple_of(n * tile, tile), tile)

    def project_first():
        load_w(0).wait()
        part = pl.ds(0, depth)

        def one(n, _):
            acc[n] = dot(attn[:, part], wb[part, columns(n)], (1, 0))
            return 0

        lax.fori_loop(0, tiles, one, 0)

    pairs = heads // 2

    def arrived(j):
        for h in (2 * j, 2 * j + 1):
            load(k_hbm, kb, k_sem, h).wait()
            load(v_hbm, vb, v_sem, h).wait()

    def update_pair(j):
        for h in (2 * j, 2 * j + 1):
            update(h)

    def begin_pair(j):
        for h in (2 * j, 2 * j + 1):
            x_line.begin(own, h)

    def lead(j, _):
        arrived(j)
        update_pair(j)
        begin_pair(j)
        return 0

    lax.fori_loop(0, LEAD, lead, 0)

    def within(j):
        return jnp.logical_and(j >= 0, j < pairs)

    def step(i, _):
        @pl.when(i < pairs)
        def _():
            for h in (2 * i, 2 * i + 1):
                x_line.finish(own, before, row_sum, h, False)
                y_line.begin(row_sum, h)
            for h in (2 * i, 2 * i + 1):
                load(q_hbm, qb, q_sem, h).wait()

        @pl.when(i < pairs - LEAD)
        def _():
            arrived(i + LEAD)
            update_pair(i + LEAD)
            begin_pair(i + LEAD)

        @pl.when(i < pairs)
        def _():
            for h in (2 * i, 2 * i + 1):
                local(h)

        @pl.when(within(i - 1))
        def _():
            for h in (2 * i - 2, 2 * i - 1):
                y_line.finish(row_sum, before, plane_sum, h, True)

                @pl.when(z == 0)
                def _():
                    z_copy(plane_sum, h).start()

        @pl.when(within(i - 1 - z))
        def _():
            j = i - 1 - z
            pair = (2 * j, 2 * j + 1)
            for h in pair:
                z_stage(h)
            for h in pair:
                read(h)

            @pl.when(j == GROUP // 2 - 1)
            def _():
                project_first()
        return 0

    lax.fori_loop(0, pairs + z_size, step, 0)

    last = pl.ds((groups - 1) * depth, depth)
    load_w(groups - 1).wait()
    theirs = pl.ds(pl.multiple_of(other * half, half), half)
    mine = pl.ds(pl.multiple_of(core * half, half), half)

    def to_peer(n):
        return pltpu.make_async_remote_copy(
            acc.at[n, theirs, :], peer.at[n], peer_send.at[n], peer_recv.at[n],
            device_id=(seq, other), device_id_type=MESH)

    def result(n):
        return pltpu.make_async_copy(outb.at[:, columns(n)], o_hbm.at[:, columns(n)], o_sem.at[n])

    def send_tile(n, _):
        acc[n, theirs, :] = acc[n, theirs, :] + dot(attn[theirs, last], wb[last, columns(n)], (1, 0))
        to_peer(n).start()
        return 0

    def own_tile(n, _):
        value = acc[n, mine, :] + dot(attn[mine, last], wb[last, columns(n)], (1, 0))
        to_peer(n).wait_recv()
        outb[:, columns(n)] = (value + peer[n]).astype(BF16)
        result(n).start()
        return 0

    lax.fori_loop(0, tiles, send_tile, 0)
    lax.fori_loop(0, tiles, own_tile, 0)

    def drain(h, _):
        x_line.drain(own, h)
        y_line.drain(row_sum, h)

        @pl.when(z < z_size - 1)
        def _():
            z_copy(plane_sum, h).wait_send()
        return 0

    def drain_tiles(n, _):
        to_peer(n).wait_send()
        result(n).wait()
        return 0

    lax.fori_loop(0, heads, drain, 0)
    lax.fori_loop(0, tiles, drain_tiles, 0)


def on_device(sizes, queries, keys, values, gate_bias, out_weight):
    heads = gate_bias.shape[0]
    rows, feat = queries.shape
    width = feat // heads
    model = out_weight.shape[1]
    tile = 512
    tiles = model // tile
    state = (width + 8, width)
    box = pltpu.VMEM((heads,) + state, F32)
    sem = pltpu.SemaphoreType.DMA((heads,))
    tile_sem = pltpu.SemaphoreType.DMA((tiles,))
    blocks = pltpu.VMEM((heads, rows, width), BF16)
    scratch = [
        blocks, blocks, blocks,
        pltpu.VMEM((heads, width + PAD, rows), BF16),
        pltpu.VMEM(out_weight.shape, BF16),
        pltpu.VMEM((heads, width, rows), F32),
        pltpu.VMEM((rows, feat), BF16),
        pltpu.VMEM((tiles, rows, tile), F32),
        pltpu.VMEM((tiles, rows // 2, tile), F32),
        pltpu.VMEM((rows // 2, model), BF16),
        box, box, box, box, box,
        sem, sem, sem, pltpu.SemaphoreType.DMA((heads // GROUP,)), tile_sem,
        sem, sem, tile_sem, tile_sem,
    ] + line_scratch(sizes[0], heads, state) + line_scratch(sizes[1], heads, state)
    hbm = pl.BlockSpec(memory_space=pl.ANY)
    return pl.pallas_call(
        functools.partial(kernel, sizes, tile),
        out_shape=jax.ShapeDtypeStruct((rows // 2, model), BF16),
        in_specs=[pl.BlockSpec(memory_space=pltpu.SMEM), hbm, hbm, hbm, hbm],
        out_specs=hbm,
        scratch_shapes=scratch,
        compiler_params=pltpu.CompilerParams(
            collective_id=0, has_side_effects=True, vmem_limit_bytes=62 * 1024 * 1024),
        cost_estimate=pl.CostEstimate(
            flops=2 * rows * feat * (model + rows + 2 * width), bytes_accessed=24 * 1024 * 1024,
            transcendentals=heads * rows * rows),
    )(gate_bias, queries, keys, values, out_weight)


def grid_of(count):
    z_size = min(4, count)
    plane = count // z_size
    y_size = 1
    while y_size * y_size < plane:
        y_size *= 2
    return (plane // y_size, y_size, z_size)


def solution(mesh):
    in_specs = (P("seq", "head"), P("seq", "head"), P("seq", "head"), P("head"), P("head", None))
    out_specs = P(("seq", "head"), None)
    return jax.shard_map(
        functools.partial(on_device, grid_of(mesh.shape["seq"])),
        mesh=mesh, in_specs=in_specs, out_specs=out_specs, check_vma=False
    )
```

```python
import functools

import jax
import jax.numpy as jnp
from jax import lax
from jax.experimental import pallas as pl
from jax.experimental.pallas import tpu as pltpu
from jax.sharding import PartitionSpec as P

SEG = 512
MESH = pl.DeviceIdType.MESH
F32 = jnp.float32
BF16 = jnp.bfloat16


def lifted(source):
    return jnp.where(source > 0, source + 1.0, jnp.exp(jnp.minimum(source, 0.0)))


def dot(a, b, dims):
    return lax.dot_general(a, b, ((dims[:1], dims[1:]), ((), ())), preferred_element_type=F32)


class Line:
    def __init__(self, size, place, device, refs):
        self.size, self.place, self.device = size, place, device
        if size == 2:
            self.inbox, self.send, self.recv = refs
        else:
            (self.right_in, self.left_in, self.right_out, self.left_out,
             self.right_send, self.right_recv, self.left_send, self.left_recv) = refs

    def swap(self, src, h):
        return pltpu.make_async_remote_copy(
            src.at[h], self.inbox.at[h], self.send.at[h], self.recv.at[h],
            device_id=self.device(1 - self.place), device_id_type=MESH)

    def to_right(self, src, h):
        return pltpu.make_async_remote_copy(
            src.at[h], self.right_in.at[h], self.right_send.at[h], self.right_recv.at[h],
            device_id=self.device(jnp.minimum(self.place + 1, self.size - 1)), device_id_type=MESH)

    def to_left(self, src, h):
        return pltpu.make_async_remote_copy(
            src.at[h], self.left_in.at[h], self.left_send.at[h], self.left_recv.at[h],
            device_id=self.device(jnp.maximum(self.place - 1, 0)), device_id_type=MESH)

    def begin(self, src, h):
        if self.size == 2:
            self.swap(src, h).start()
            return

        @pl.when(self.place == 0)
        def _():
            self.to_right(src, h).start()

        @pl.when(self.place == self.size - 1)
        def _():
            self.to_left(src, h).start()

    def finish(self, src, before, total, h, add):
        if self.size == 2:
            self.swap(src, h).wait_recv()
            got = self.inbox[h]
            total[h] = src[h] + got
            earlier = jnp.where(self.place > 0, got, jnp.zeros_like(got))
            before[h] = before[h] + earlier if add else earlier
            return
        place, last = self.place, self.size - 1
        total[h] = src[h]
        if not add:
            before[h] = jnp.zeros(before.shape[1:], F32)

        @pl.when(place > 0)
        def _():
            self.to_right(src, h).wait_recv()
            got = self.right_in[h]
            before[h] = before[h] + got
            total[h] = total[h] + got

            @pl.when(place < last)
            def _():
                self.right_out[h] = got + src[h]
                self.to_right(self.right_out, h).start()

        @pl.when(place < last)
        def _():
            self.to_left(src, h).wait_recv()
            got = self.left_in[h]
            total[h] = total[h] + got

            @pl.when(place > 0)
            def _():
                self.left_out[h] = got + src[h]
                self.to_left(self.left_out, h).start()

    def drain(self, src, h):
        if self.size == 2:
            self.swap(src, h).wait_send()
            return

        @pl.when(self.place < self.size - 1)
        def _():
            self.to_right(src, h).wait_send()

        @pl.when(self.place > 0)
        def _():
            self.to_left(src, h).wait_send()


def line_scratch(size, heads, state):
    box = pltpu.VMEM((heads,) + state, F32)
    sem = pltpu.SemaphoreType.DMA((heads,))
    return [box, sem, sem] if size == 2 else [box] * 4 + [sem] * 4


GROUP = 8
PAD = 16
LEAD = 4


def kernel(sizes, tile, gate, q_hbm, k_hbm, v_hbm, w_hbm, o_hbm, *scratch):
    x_size, y_size, z_size = sizes
    scratch = list(scratch)

    def take(count):
        taken = scratch[:count]
        del scratch[:count]
        return taken

    qb, kb, vb, vt, wb, loc, attn, acc, peer, outb = take(10)
    own, row_sum, plane_sum, before, z_in = take(5)
    q_sem, k_sem, v_sem, w_sem, o_sem = take(5)
    z_send, z_recv, peer_send, peer_recv = take(4)
    x_refs = take(3 if x_size == 2 else 8)
    y_refs = take(3 if y_size == 2 else 8)

    heads, rows, width = qb.shape
    half = rows // 2
    tiles = acc.shape[0]
    depth = GROUP * width
    groups = heads // GROUP
    seq, core = lax.axis_index("seq"), lax.axis_index("head")
    x = lax.rem(seq, x_size)
    y = lax.rem(seq // x_size, y_size)
    z = seq // (x_size * y_size)

    def at(xx, yy, zz):
        return ((zz * y_size + yy) * x_size + xx, core)

    x_line = Line(x_size, x, lambda c: at(c, y, z), x_refs)
    y_line = Line(y_size, y, lambda c: at(x, c, z), y_refs)
    other = 1 - core

    def load(src, dst, sem, h):
        return pltpu.make_async_copy(
            src.at[:, pl.ds(pl.multiple_of(h * width, width), width)], dst.at[h], sem.at[h])

    def load_w(g):
        part = pl.ds(pl.multiple_of(g * depth, depth), depth)
        return pltpu.make_async_copy(w_hbm.at[part, :], wb.at[part, :], w_sem.at[g])

    def start_loads(h, _):
        load(k_hbm, kb, k_sem, h).start()
        load(v_hbm, vb, v_sem, h).start()
        return 0

    def start_queries(h, _):
        load(q_hbm, qb, q_sem, h).start()
        return 0

    def start_weights(g, _):
        load_w(g).start()
        return 0

    lax.fori_loop(0, LEAD, start_loads, 0)

    barrier = pltpu.get_barrier_semaphore()
    pl.semaphore_signal(barrier, inc=1, device_id=(seq, other), device_id_type=MESH)
    greeted = 1
    for place, size, where in (
        (x, x_size, lambda c: at(c, y, z)),
        (y, y_size, lambda c: at(x, c, z)),
        (z, z_size, lambda c: at(x, y, c)),
    ):
        @pl.when(place > 0)
        def _():
            pl.semaphore_signal(barrier, inc=1, device_id=where(place - 1), device_id_type=MESH)

        @pl.when(place < size - 1)
        def _():
            pl.semaphore_signal(barrier, inc=1, device_id=where(place + 1), device_id_type=MESH)

        greeted = greeted + (place > 0).astype(jnp.int32) + (place < size - 1).astype(jnp.int32)
    pl.semaphore_wait(barrier, greeted)

    def z_copy(src, h):
        return pltpu.make_async_remote_copy(
            src.at[h], z_in.at[h], z_send.at[h], z_recv.at[h],
            device_id=at(x, y, jnp.minimum(z + 1, z_size - 1)), device_id_type=MESH)

    def update(h):
        lift_key = lifted(kb[h].astype(F32)).astype(BF16)
        vt[h, pl.ds(0, width), :] = vb[h].T
        vt[h, pl.ds(width, PAD), :] = jnp.ones((PAD, rows), BF16)
        own[h] = dot(vt[h], lift_key, (1, 0))[:width + 8]

    def local(h):
        rate = 1.4426950408889634 / (width ** 0.5)
        keep = 1.0 / (1.0 + jnp.exp(jnp.full((1, half), gate[h], F32)))
        causal = (lax.broadcasted_iota(jnp.int32, (half, half), 0)
                  <= lax.broadcasted_iota(jnp.int32, (half, half), 1))
        for part in range(2):
            here = pl.ds(part * half, half)
            qs = qb[h, here, :]
            diag = jnp.where(causal, dot(kb[h, here, :], qs, (1, 1)), -jnp.inf)
            top = jnp.max(diag, axis=0, keepdims=True)
            if part == 1:
                past = dot(kb[h, pl.ds(0, half), :], qs, (1, 1))
                top = jnp.maximum(top, jnp.max(past, axis=0, keepdims=True))
                past = jnp.exp2((past - top) * rate)
            diag = jnp.exp2((diag - top) * rate)
            total = jnp.sum(diag, axis=0, keepdims=True)
            if part == 1:
                total = total + jnp.sum(past, axis=0, keepdims=True)
            inverse = 1.0 / total
            out = dot(vt[h, pl.ds(0, width), here], (diag * inverse).astype(BF16), (1, 0))
            if part == 1:
                out = out + dot(vt[h, pl.ds(0, width), pl.ds(0, half)], (past * inverse).astype(BF16), (1, 0))
            loc[h, :, here] = out * keep

    def z_stage(h):
        @pl.when(z > 0)
        def _():
            z_copy(plane_sum, h).wait_recv()
            got = z_in[h]
            before[h] = before[h] + got

            @pl.when(z < z_size - 1)
            def _():
                plane_sum[h] = plane_sum[h] + got
                z_copy(plane_sum, h).start()

    def read(h):
        share = 1.0 / (1.0 + jnp.exp(jnp.full((1, rows), -gate[h], F32)))
        lift_query = lifted(qb[h].astype(F32)).astype(BF16)
        norm = before[h, pl.ds(width, 1), :]
        high = norm.astype(BF16).astype(F32)
        middle = (norm - high).astype(BF16).astype(F32)
        low = norm - high - middle
        row = lax.broadcasted_iota(jnp.int32, (PAD, width), 0)
        parts = jnp.where(row == 0, high, jnp.where(row == 1, middle, jnp.where(row == 2, low, 0.0)))
        memory = before[h, pl.ds(0, width), :].astype(BF16)
        got = dot(jnp.concatenate([memory, parts.astype(BF16)], axis=0), lift_query, (1, 1))
        denominator = jnp.sum(got[width:width + 8], axis=0, keepdims=True)
        value = got[:width] * (share / jnp.maximum(denominator, 1.0)) + loc[h]
        attn[:, pl.ds(pl.multiple_of(h * width, width), width)] = value.astype(BF16).T

    def columns(n):
        return pl.ds(pl.multiple_of(n * tile, tile), tile)

    def project_first():
        load_w(0).wait()
        part = pl.ds(0, depth)

        def one(n, _):
            acc[n] = dot(attn[:, part], wb[part, columns(n)], (1, 0))
            return 0

        lax.fori_loop(0, tiles, one, 0)

    def update_pair(first):
        for h in (first, first + 1):
            load(k_hbm, kb, k_sem, h).wait()
            load(v_hbm, vb, v_sem, h).wait()
        for h in (first, first + 1):
            update(h)

    update_pair(0)
    x_line.begin(own, 0)
    x_line.begin(own, 1)
    lax.fori_loop(LEAD, heads, start_loads, 0)
    lax.fori_loop(0, heads, start_queries, 0)
    lax.fori_loop(0, groups, start_weights, 0)
    update_pair(2)

    def within(h):
        return jnp.logical_and(h >= 0, h < heads)

    def step(t, _):
        even = lax.rem(t, 2) == 0

        @pl.when(t < heads)
        def _():
            x_line.finish(own, before, row_sum, t, False)
            y_line.begin(row_sum, t)

        @pl.when(t < heads - 2)
        def _():
            x_line.begin(own, t + 2)

        @pl.when(within(t - 2))
        def _():
            y_line.finish(row_sum, before, plane_sum, t - 2, True)

            @pl.when(z == 0)
            def _():
                z_copy(plane_sum, t - 2).start()

        h = t - 2 - z

        @pl.when(within(h))
        def _():
            z_stage(h)

        @pl.when(jnp.logical_and(even, t < heads))
        def _():
            for head in (t, t + 1):
                load(q_hbm, qb, q_sem, head).wait()
            for head in (t, t + 1):
                local(head)

        @pl.when(jnp.logical_and(jnp.logical_not(even), t < heads - LEAD))
        def _():
            update_pair(t + 3)

        @pl.when(jnp.logical_and(within(h), lax.rem(h, 2) == 1))
        def _():
            read(h - 1)
            read(h)

            @pl.when(h == GROUP - 1)
            def _():
                project_first()
        return 0

    lax.fori_loop(0, heads + 1 + z_size, step, 0)

    last = pl.ds((groups - 1) * depth, depth)
    load_w(groups - 1).wait()
    theirs = pl.ds(pl.multiple_of(other * half, half), half)
    mine = pl.ds(pl.multiple_of(core * half, half), half)

    def to_peer(n):
        return pltpu.make_async_remote_copy(
            acc.at[n, theirs, :], peer.at[n], peer_send.at[n], peer_recv.at[n],
            device_id=(seq, other), device_id_type=MESH)

    def result(n):
        return pltpu.make_async_copy(outb.at[:, columns(n)], o_hbm.at[:, columns(n)], o_sem.at[n])

    def send_tile(n, _):
        acc[n, theirs, :] = acc[n, theirs, :] + dot(attn[theirs, last], wb[last, columns(n)], (1, 0))
        to_peer(n).start()
        return 0

    def own_tile(n, _):
        value = acc[n, mine, :] + dot(attn[mine, last], wb[last, columns(n)], (1, 0))
        to_peer(n).wait_recv()
        outb[:, columns(n)] = (value + peer[n]).astype(BF16)
        result(n).start()
        return 0

    lax.fori_loop(0, tiles, send_tile, 0)
    lax.fori_loop(0, tiles, own_tile, 0)

    def drain(h, _):
        x_line.drain(own, h)
        y_line.drain(row_sum, h)

        @pl.when(z < z_size - 1)
        def _():
            z_copy(plane_sum, h).wait_send()
        return 0

    def drain_tiles(n, _):
        to_peer(n).wait_send()
        result(n).wait()
        return 0

    lax.fori_loop(0, heads, drain, 0)
    lax.fori_loop(0, tiles, drain_tiles, 0)


def on_device(sizes, queries, keys, values, gate_bias, out_weight):
    heads = gate_bias.shape[0]
    rows, feat = queries.shape
    width = feat // heads
    model = out_weight.shape[1]
    tile = 512
    tiles = model // tile
    state = (width + 8, width)
    box = pltpu.VMEM((heads,) + state, F32)
    sem = pltpu.SemaphoreType.DMA((heads,))
    tile_sem = pltpu.SemaphoreType.DMA((tiles,))
    blocks = pltpu.VMEM((heads, rows, width), BF16)
    scratch = [
        blocks, blocks, blocks,
        pltpu.VMEM((heads, width + PAD, rows), BF16),
        pltpu.VMEM(out_weight.shape, BF16),
        pltpu.VMEM((heads, width, rows), F32),
        pltpu.VMEM((rows, feat), BF16),
        pltpu.VMEM((tiles, rows, tile), F32),
        pltpu.VMEM((tiles, rows // 2, tile), F32),
        pltpu.VMEM((rows // 2, model), BF16),
        box, box, box, box, box,
        sem, sem, sem, pltpu.SemaphoreType.DMA((heads // GROUP,)), tile_sem,
        sem, sem, tile_sem, tile_sem,
    ] + line_scratch(sizes[0], heads, state) + line_scratch(sizes[1], heads, state)
    hbm = pl.BlockSpec(memory_space=pl.ANY)
    return pl.pallas_call(
        functools.partial(kernel, sizes, tile),
        out_shape=jax.ShapeDtypeStruct((rows // 2, model), BF16),
        in_specs=[pl.BlockSpec(memory_space=pltpu.SMEM), hbm, hbm, hbm, hbm],
        out_specs=hbm,
        scratch_shapes=scratch,
        compiler_params=pltpu.CompilerParams(
            collective_id=0, has_side_effects=True, vmem_limit_bytes=62 * 1024 * 1024),
        cost_estimate=pl.CostEstimate(
            flops=2 * rows * feat * (model + rows + 2 * width), bytes_accessed=24 * 1024 * 1024,
            transcendentals=heads * rows * rows),
    )(gate_bias, queries, keys, values, out_weight)


def grid_of(count):
    z_size = min(4, count)
    plane = count // z_size
    y_size = 1
    while y_size * y_size < plane:
        y_size *= 2
    return (plane // y_size, y_size, z_size)


def solution(mesh):
    in_specs = (P("seq", "head"), P("seq", "head"), P("seq", "head"), P("head"), P("head", None))
    out_specs = P(("seq", "head"), None)
    return jax.shard_map(
        functools.partial(on_device, grid_of(mesh.shape["seq"])),
        mesh=mesh, in_specs=in_specs, out_specs=out_specs, check_vma=False
    )
```

```python
import functools

import jax
import jax.numpy as jnp
from jax import lax
from jax.experimental import pallas as pl
from jax.experimental.pallas import tpu as pltpu
from jax.sharding import PartitionSpec as P

SEG = 512
MESH = pl.DeviceIdType.MESH
F32 = jnp.float32
BF16 = jnp.bfloat16


def lifted(source):
    return jnp.where(source > 0, source + 1.0, jnp.exp(jnp.minimum(source, 0.0)))


def dot(a, b, dims):
    return lax.dot_general(a, b, ((dims[:1], dims[1:]), ((), ())), preferred_element_type=F32)


class Line:
    def __init__(self, size, place, device, refs):
        self.size, self.place, self.device = size, place, device
        if size == 2:
            self.inbox, self.send, self.recv = refs
        else:
            (self.right_in, self.left_in, self.right_out, self.left_out,
             self.right_send, self.right_recv, self.left_send, self.left_recv) = refs

    def swap(self, src, h):
        return pltpu.make_async_remote_copy(
            src.at[h], self.inbox.at[h], self.send.at[h], self.recv.at[h],
            device_id=self.device(1 - self.place), device_id_type=MESH)

    def to_right(self, src, h):
        return pltpu.make_async_remote_copy(
            src.at[h], self.right_in.at[h], self.right_send.at[h], self.right_recv.at[h],
            device_id=self.device(jnp.minimum(self.place + 1, self.size - 1)), device_id_type=MESH)

    def to_left(self, src, h):
        return pltpu.make_async_remote_copy(
            src.at[h], self.left_in.at[h], self.left_send.at[h], self.left_recv.at[h],
            device_id=self.device(jnp.maximum(self.place - 1, 0)), device_id_type=MESH)

    def begin(self, src, h):
        if self.size == 2:
            self.swap(src, h).start()
            return

        @pl.when(self.place == 0)
        def _():
            self.to_right(src, h).start()

        @pl.when(self.place == self.size - 1)
        def _():
            self.to_left(src, h).start()

    def finish(self, src, before, total, h, add):
        if self.size == 2:
            self.swap(src, h).wait_recv()
            got = self.inbox[h]
            total[h] = src[h] + got
            earlier = jnp.where(self.place > 0, got, jnp.zeros_like(got))
            before[h] = before[h] + earlier if add else earlier
            return
        place, last = self.place, self.size - 1
        total[h] = src[h]
        if not add:
            before[h] = jnp.zeros(before.shape[1:], F32)

        @pl.when(place > 0)
        def _():
            self.to_right(src, h).wait_recv()
            got = self.right_in[h]
            before[h] = before[h] + got
            total[h] = total[h] + got

            @pl.when(place < last)
            def _():
                self.right_out[h] = got + src[h]
                self.to_right(self.right_out, h).start()

        @pl.when(place < last)
        def _():
            self.to_left(src, h).wait_recv()
            got = self.left_in[h]
            total[h] = total[h] + got

            @pl.when(place > 0)
            def _():
                self.left_out[h] = got + src[h]
                self.to_left(self.left_out, h).start()

    def drain(self, src, h):
        if self.size == 2:
            self.swap(src, h).wait_send()
            return

        @pl.when(self.place < self.size - 1)
        def _():
            self.to_right(src, h).wait_send()

        @pl.when(self.place > 0)
        def _():
            self.to_left(src, h).wait_send()


def line_scratch(size, heads, state):
    box = pltpu.VMEM((heads,) + state, F32)
    sem = pltpu.SemaphoreType.DMA((heads,))
    return [box, sem, sem] if size == 2 else [box] * 4 + [sem] * 4


GROUP = 8
PAD = 16
LEAD = 6


def kernel(sizes, tile, gate, q_hbm, k_hbm, v_hbm, w_hbm, o_hbm, *scratch):
    x_size, y_size, z_size = sizes
    scratch = list(scratch)

    def take(count):
        taken = scratch[:count]
        del scratch[:count]
        return taken

    qb, kb, vb, vt, wb, loc, attn, acc, peer, outb = take(10)
    own, row_sum, plane_sum, before, z_in = take(5)
    q_sem, k_sem, v_sem, w_sem, o_sem = take(5)
    z_send, z_recv, peer_send, peer_recv = take(4)
    x_refs = take(3 if x_size == 2 else 8)
    y_refs = take(3 if y_size == 2 else 8)

    heads, rows, width = qb.shape
    half = rows // 2
    tiles = acc.shape[0]
    depth = GROUP * width
    groups = heads // GROUP
    seq, core = lax.axis_index("seq"), lax.axis_index("head")
    x = lax.rem(seq, x_size)
    y = lax.rem(seq // x_size, y_size)
    z = seq // (x_size * y_size)

    def at(xx, yy, zz):
        return ((zz * y_size + yy) * x_size + xx, core)

    x_line = Line(x_size, x, lambda c: at(c, y, z), x_refs)
    y_line = Line(y_size, y, lambda c: at(x, c, z), y_refs)
    other = 1 - core

    def load(src, dst, sem, h):
        return pltpu.make_async_copy(
            src.at[:, pl.ds(pl.multiple_of(h * width, width), width)], dst.at[h], sem.at[h])

    def load_w(g):
        part = pl.ds(pl.multiple_of(g * depth, depth), depth)
        return pltpu.make_async_copy(w_hbm.at[part, :], wb.at[part, :], w_sem.at[g])

    def start_loads(h, _):
        load(k_hbm, kb, k_sem, h).start()
        load(v_hbm, vb, v_sem, h).start()
        return 0

    def start_queries(h, _):
        load(q_hbm, qb, q_sem, h).start()
        return 0

    def start_weights(g, _):
        load_w(g).start()
        return 0

    lax.fori_loop(0, LEAD, start_loads, 0)

    barrier = pltpu.get_barrier_semaphore()
    pl.semaphore_signal(barrier, inc=1, device_id=(seq, other), device_id_type=MESH)
    greeted = 1
    for place, size, where in (
        (x, x_size, lambda c: at(c, y, z)),
        (y, y_size, lambda c: at(x, c, z)),
        (z, z_size, lambda c: at(x, y, c)),
    ):
        @pl.when(place > 0)
        def _():
            pl.semaphore_signal(barrier, inc=1, device_id=where(place - 1), device_id_type=MESH)

        @pl.when(place < size - 1)
        def _():
            pl.semaphore_signal(barrier, inc=1, device_id=where(place + 1), device_id_type=MESH)

        greeted = greeted + (place > 0).astype(jnp.int32) + (place < size - 1).astype(jnp.int32)
    pl.semaphore_wait(barrier, greeted)

    cut = width // 2
    pieces = ((0, pl.ds(0, cut)), (1, pl.ds(cut, width + 8 - cut)))

    def z_copy(src, h, piece):
        index, part = piece
        return pltpu.make_async_remote_copy(
            src.at[h, part, :], z_in.at[h, part, :], z_send.at[index, h], z_recv.at[index, h],
            device_id=at(x, y, jnp.minimum(z + 1, z_size - 1)), device_id_type=MESH)

    def update(h):
        lift_key = lifted(kb[h].astype(F32)).astype(BF16)
        vt[h, pl.ds(0, width), :] = vb[h].T
        vt[h, pl.ds(width, PAD), :] = jnp.ones((PAD, rows), BF16)
        own[h] = dot(vt[h], lift_key, (1, 0))[:width + 8]

    def local(h):
        rate = 1.4426950408889634 / (width ** 0.5)
        keep = 1.0 / (1.0 + jnp.exp(jnp.full((1, half), gate[h], F32)))
        causal = (lax.broadcasted_iota(jnp.int32, (half, half), 0)
                  <= lax.broadcasted_iota(jnp.int32, (half, half), 1))
        for part in range(2):
            here = pl.ds(part * half, half)
            qs = qb[h, here, :]
            diag = jnp.where(causal, dot(kb[h, here, :], qs, (1, 1)), -jnp.inf)
            top = jnp.max(diag, axis=0, keepdims=True)
            if part == 1:
                past = dot(kb[h, pl.ds(0, half), :], qs, (1, 1))
                top = jnp.maximum(top, jnp.max(past, axis=0, keepdims=True))
                past = jnp.exp2((past - top) * rate)
            diag = jnp.exp2((diag - top) * rate)
            total = jnp.sum(diag, axis=0, keepdims=True)
            if part == 1:
                total = total + jnp.sum(past, axis=0, keepdims=True)
            inverse = 1.0 / total
            out = dot(vt[h, pl.ds(0, width), here], (diag * inverse).astype(BF16), (1, 0))
            if part == 1:
                out = out + dot(vt[h, pl.ds(0, width), pl.ds(0, half)], (past * inverse).astype(BF16), (1, 0))
            loc[h, :, here] = out * keep

    def z_stage(h):
        @pl.when(z > 0)
        def _():
            for piece in pieces:
                part = piece[1]
                z_copy(plane_sum, h, piece).wait_recv()
                got = z_in[h, part, :]
                before[h, part, :] = before[h, part, :] + got

                @pl.when(z < z_size - 1)
                def _():
                    plane_sum[h, part, :] = plane_sum[h, part, :] + got
                    z_copy(plane_sum, h, piece).start()

    def read(h):
        share = 1.0 / (1.0 + jnp.exp(jnp.full((1, rows), -gate[h], F32)))
        lift_query = lifted(qb[h].astype(F32)).astype(BF16)
        norm = before[h, pl.ds(width, 1), :]
        high = norm.astype(BF16).astype(F32)
        middle = (norm - high).astype(BF16).astype(F32)
        low = norm - high - middle
        row = lax.broadcasted_iota(jnp.int32, (PAD, width), 0)
        parts = jnp.where(row == 0, high, jnp.where(row == 1, middle, jnp.where(row == 2, low, 0.0)))
        memory = before[h, pl.ds(0, width), :].astype(BF16)
        got = dot(jnp.concatenate([memory, parts.astype(BF16)], axis=0), lift_query, (1, 1))
        denominator = jnp.sum(got[width:width + 8], axis=0, keepdims=True)
        value = got[:width] * (share / jnp.maximum(denominator, 1.0)) + loc[h]
        attn[:, pl.ds(pl.multiple_of(h * width, width), width)] = value.astype(BF16).T

    def columns(n):
        return pl.ds(pl.multiple_of(n * tile, tile), tile)

    def project_first():
        load_w(0).wait()
        part = pl.ds(0, depth)

        def one(n, _):
            acc[n] = dot(attn[:, part], wb[part, columns(n)], (1, 0))
            return 0

        lax.fori_loop(0, tiles, one, 0)

    def update_pair(first):
        for h in (first, first + 1):
            load(k_hbm, kb, k_sem, h).wait()
            load(v_hbm, vb, v_sem, h).wait()
        for h in (first, first + 1):
            update(h)

    update_pair(0)
    x_line.begin(own, 0)
    x_line.begin(own, 1)
    lax.fori_loop(LEAD, heads, start_loads, 0)
    lax.fori_loop(0, heads, start_queries, 0)
    lax.fori_loop(0, groups, start_weights, 0)
    update_pair(2)
    x_line.begin(own, 2)
    x_line.begin(own, 3)
    update_pair(4)

    def within(h):
        return jnp.logical_and(h >= 0, h < heads)

    def step(t, _):
        even = lax.rem(t, 2) == 0

        @pl.when(t < heads)
        def _():
            x_line.finish(own, before, row_sum, t, False)
            y_line.begin(row_sum, t)

        @pl.when(t < heads - 4)
        def _():
            x_line.begin(own, t + 4)

        @pl.when(within(t - 2))
        def _():
            y_line.finish(row_sum, before, plane_sum, t - 2, True)

            @pl.when(z == 0)
            def _():
                for piece in pieces:
                    z_copy(plane_sum, t - 2, piece).start()

        h = t - 2 - z

        @pl.when(within(h))
        def _():
            z_stage(h)

        @pl.when(jnp.logical_and(even, t < heads))
        def _():
            for head in (t, t + 1):
                load(q_hbm, qb, q_sem, head).wait()
            for head in (t, t + 1):
                local(head)

        @pl.when(jnp.logical_and(jnp.logical_not(even), t < heads - LEAD))
        def _():
            update_pair(t + 5)

        @pl.when(jnp.logical_and(within(h), lax.rem(h, 2) == 1))
        def _():
            read(h - 1)
            read(h)

            @pl.when(h == GROUP - 1)
            def _():
                project_first()
        return 0

    lax.fori_loop(0, heads + 1 + z_size, step, 0)

    last = pl.ds((groups - 1) * depth, depth)
    load_w(groups - 1).wait()
    theirs = pl.ds(pl.multiple_of(other * half, half), half)
    mine = pl.ds(pl.multiple_of(core * half, half), half)

    def to_peer(n):
        return pltpu.make_async_remote_copy(
            acc.at[n, theirs, :], peer.at[n], peer_send.at[n], peer_recv.at[n],
            device_id=(seq, other), device_id_type=MESH)

    def result(n):
        return pltpu.make_async_copy(outb.at[:, columns(n)], o_hbm.at[:, columns(n)], o_sem.at[n])

    def send_tile(n, _):
        acc[n, theirs, :] = acc[n, theirs, :] + dot(attn[theirs, last], wb[last, columns(n)], (1, 0))
        to_peer(n).start()
        return 0

    def own_tile(n, _):
        value = acc[n, mine, :] + dot(attn[mine, last], wb[last, columns(n)], (1, 0))
        to_peer(n).wait_recv()
        outb[:, columns(n)] = (value + peer[n]).astype(BF16)
        result(n).start()
        return 0

    lax.fori_loop(0, tiles, send_tile, 0)
    lax.fori_loop(0, tiles, own_tile, 0)

    def drain(h, _):
        x_line.drain(own, h)
        y_line.drain(row_sum, h)

        @pl.when(z < z_size - 1)
        def _():
            for piece in pieces:
                z_copy(plane_sum, h, piece).wait_send()
        return 0

    def drain_tiles(n, _):
        to_peer(n).wait_send()
        result(n).wait()
        return 0

    lax.fori_loop(0, heads, drain, 0)
    lax.fori_loop(0, tiles, drain_tiles, 0)


def on_device(sizes, queries, keys, values, gate_bias, out_weight):
    heads = gate_bias.shape[0]
    rows, feat = queries.shape
    width = feat // heads
    model = out_weight.shape[1]
    tile = 512
    tiles = model // tile
    state = (width + 8, width)
    box = pltpu.VMEM((heads,) + state, F32)
    sem = pltpu.SemaphoreType.DMA((heads,))
    tile_sem = pltpu.SemaphoreType.DMA((tiles,))
    blocks = pltpu.VMEM((heads, rows, width), BF16)
    scratch = [
        blocks, blocks, blocks,
        pltpu.VMEM((heads, width + PAD, rows), BF16),
        pltpu.VMEM(out_weight.shape, BF16),
        pltpu.VMEM((heads, width, rows), F32),
        pltpu.VMEM((rows, feat), BF16),
        pltpu.VMEM((tiles, rows, tile), F32),
        pltpu.VMEM((tiles, rows // 2, tile), F32),
        pltpu.VMEM((rows // 2, model), BF16),
        box, box, box, box, box,
        sem, sem, sem, pltpu.SemaphoreType.DMA((heads // GROUP,)), tile_sem,
        pltpu.SemaphoreType.DMA((2, heads)), pltpu.SemaphoreType.DMA((2, heads)), tile_sem, tile_sem,
    ] + line_scratch(sizes[0], heads, state) + line_scratch(sizes[1], heads, state)
    hbm = pl.BlockSpec(memory_space=pl.ANY)
    return pl.pallas_call(
        functools.partial(kernel, sizes, tile),
        out_shape=jax.ShapeDtypeStruct((rows // 2, model), BF16),
        in_specs=[pl.BlockSpec(memory_space=pltpu.SMEM), hbm, hbm, hbm, hbm],
        out_specs=hbm,
        scratch_shapes=scratch,
        compiler_params=pltpu.CompilerParams(
            collective_id=0, has_side_effects=True, vmem_limit_bytes=62 * 1024 * 1024),
        cost_estimate=pl.CostEstimate(
            flops=2 * rows * feat * (model + rows + 2 * width), bytes_accessed=24 * 1024 * 1024,
            transcendentals=heads * rows * rows),
    )(gate_bias, queries, keys, values, out_weight)


def grid_of(count):
    z_size = min(4, count)
    plane = count // z_size
    y_size = 1
    while y_size * y_size < plane:
        y_size *= 2
    return (plane // y_size, y_size, z_size)


def solution(mesh):
    in_specs = (P("seq", "head"), P("seq", "head"), P("seq", "head"), P("head"), P("head", None))
    out_specs = P(("seq", "head"), None)
    return jax.shard_map(
        functools.partial(on_device, grid_of(mesh.shape["seq"])),
        mesh=mesh, in_specs=in_specs, out_specs=out_specs, check_vma=False
    )
```

```python
import functools

import jax
import jax.numpy as jnp
from jax import lax
from jax.experimental import pallas as pl
from jax.experimental.pallas import tpu as pltpu
from jax.sharding import PartitionSpec as P

SEG = 512
MESH = pl.DeviceIdType.MESH
F32 = jnp.float32
BF16 = jnp.bfloat16


def lifted(source):
    return jnp.where(source > 0, source + 1.0, jnp.exp(jnp.minimum(source, 0.0)))


def dot(a, b, dims):
    return lax.dot_general(a, b, ((dims[:1], dims[1:]), ((), ())), preferred_element_type=F32)


class Line:
    def __init__(self, size, place, device, refs):
        self.size, self.place, self.device = size, place, device
        if size == 2:
            self.inbox, self.send, self.recv = refs
        else:
            (self.right_in, self.left_in, self.right_out, self.left_out,
             self.right_send, self.right_recv, self.left_send, self.left_recv) = refs

    def swap(self, src, h):
        return pltpu.make_async_remote_copy(
            src.at[h], self.inbox.at[h], self.send.at[h], self.recv.at[h],
            device_id=self.device(1 - self.place), device_id_type=MESH)

    def to_right(self, src, h):
        return pltpu.make_async_remote_copy(
            src.at[h], self.right_in.at[h], self.right_send.at[h], self.right_recv.at[h],
            device_id=self.device(jnp.minimum(self.place + 1, self.size - 1)), device_id_type=MESH)

    def to_left(self, src, h):
        return pltpu.make_async_remote_copy(
            src.at[h], self.left_in.at[h], self.left_send.at[h], self.left_recv.at[h],
            device_id=self.device(jnp.maximum(self.place - 1, 0)), device_id_type=MESH)

    def begin(self, src, h):
        if self.size == 2:
            self.swap(src, h).start()
            return

        @pl.when(self.place == 0)
        def _():
            self.to_right(src, h).start()

        @pl.when(self.place == self.size - 1)
        def _():
            self.to_left(src, h).start()

    def finish(self, src, before, total, h, add):
        if self.size == 2:
            self.swap(src, h).wait_recv()
            got = self.inbox[h]
            total[h] = src[h] + got
            earlier = jnp.where(self.place > 0, got, jnp.zeros_like(got))
            before[h] = before[h] + earlier if add else earlier
            return
        place, last = self.place, self.size - 1
        total[h] = src[h]
        if not add:
            before[h] = jnp.zeros(before.shape[1:], F32)

        @pl.when(place > 0)
        def _():
            self.to_right(src, h).wait_recv()
            got = self.right_in[h]
            before[h] = before[h] + got
            total[h] = total[h] + got

            @pl.when(place < last)
            def _():
                self.right_out[h] = got + src[h]
                self.to_right(self.right_out, h).start()

        @pl.when(place < last)
        def _():
            self.to_left(src, h).wait_recv()
            got = self.left_in[h]
            total[h] = total[h] + got

            @pl.when(place > 0)
            def _():
                self.left_out[h] = got + src[h]
                self.to_left(self.left_out, h).start()

    def drain(self, src, h):
        if self.size == 2:
            self.swap(src, h).wait_send()
            return

        @pl.when(self.place < self.size - 1)
        def _():
            self.to_right(src, h).wait_send()

        @pl.when(self.place > 0)
        def _():
            self.to_left(src, h).wait_send()


def line_scratch(size, heads, state):
    box = pltpu.VMEM((heads,) + state, F32)
    sem = pltpu.SemaphoreType.DMA((heads,))
    return [box, sem, sem] if size == 2 else [box] * 4 + [sem] * 4


GROUP = 8
PAD = 16
LEAD = 6


def kernel(sizes, tile, gate, q_hbm, k_hbm, v_hbm, w_hbm, o_hbm, *scratch):
    x_size, y_size, z_size = sizes
    scratch = list(scratch)

    def take(count):
        taken = scratch[:count]
        del scratch[:count]
        return taken

    qb, kb, vb, vt, wb, loc, attn, acc, peer, outb = take(10)
    own, row_sum, plane_sum, before, z_in = take(5)
    q_sem, k_sem, v_sem, w_sem, o_sem = take(5)
    z_send, z_recv, peer_send, peer_recv = take(4)
    x_refs = take(3 if x_size == 2 else 8)
    y_refs = take(3 if y_size == 2 else 8)

    heads, rows, width = qb.shape
    half = rows // 2
    tiles = acc.shape[0]
    depth = GROUP * width
    groups = heads // GROUP
    seq, core = lax.axis_index("seq"), lax.axis_index("head")
    x = lax.rem(seq, x_size)
    y = lax.rem(seq // x_size, y_size)
    z = seq // (x_size * y_size)

    def at(xx, yy, zz):
        return ((zz * y_size + yy) * x_size + xx, core)

    x_line = Line(x_size, x, lambda c: at(c, y, z), x_refs)
    y_line = Line(y_size, y, lambda c: at(x, c, z), y_refs)
    other = 1 - core

    def load(src, dst, sem, h):
        return pltpu.make_async_copy(
            src.at[:, pl.ds(pl.multiple_of(h * width, width), width)], dst.at[h], sem.at[h])

    def load_w(g):
        part = pl.ds(pl.multiple_of(g * depth, depth), depth)
        return pltpu.make_async_copy(w_hbm.at[part, :], wb.at[part, :], w_sem.at[g])

    def start_loads(h, _):
        load(k_hbm, kb, k_sem, h).start()
        load(v_hbm, vb, v_sem, h).start()
        return 0

    def start_queries(h, _):
        load(q_hbm, qb, q_sem, h).start()
        return 0

    def start_weights(g, _):
        load_w(g).start()
        return 0

    lax.fori_loop(0, LEAD, start_loads, 0)

    barrier = pltpu.get_barrier_semaphore()
    pl.semaphore_signal(barrier, inc=1, device_id=(seq, other), device_id_type=MESH)
    greeted = 1
    for place, size, where in (
        (x, x_size, lambda c: at(c, y, z)),
        (y, y_size, lambda c: at(x, c, z)),
        (z, z_size, lambda c: at(x, y, c)),
    ):
        @pl.when(place > 0)
        def _():
            pl.semaphore_signal(barrier, inc=1, device_id=where(place - 1), device_id_type=MESH)

        @pl.when(place < size - 1)
        def _():
            pl.semaphore_signal(barrier, inc=1, device_id=where(place + 1), device_id_type=MESH)

        greeted = greeted + (place > 0).astype(jnp.int32) + (place < size - 1).astype(jnp.int32)
    pl.semaphore_wait(barrier, greeted)

    cut = width // 2
    pieces = ((0, pl.ds(0, cut)), (1, pl.ds(cut, width + 8 - cut)))

    def z_copy(src, h, piece):
        index, part = piece
        return pltpu.make_async_remote_copy(
            src.at[h, part, :], z_in.at[h, part, :], z_send.at[index, h], z_recv.at[index, h],
            device_id=at(x, y, jnp.minimum(z + 1, z_size - 1)), device_id_type=MESH)

    def update(h):
        lift_key = lifted(kb[h].astype(F32)).astype(BF16)
        vt[h, pl.ds(0, width), :] = vb[h].T
        vt[h, pl.ds(width, PAD), :] = jnp.ones((PAD, rows), BF16)
        own[h] = dot(vt[h], lift_key, (1, 0))[:width + 8]

    def local(h):
        rate = 1.4426950408889634 / (width ** 0.5)
        keep = 1.0 / (1.0 + jnp.exp(jnp.full((1, half), gate[h], F32)))
        causal = (lax.broadcasted_iota(jnp.int32, (half, half), 0)
                  <= lax.broadcasted_iota(jnp.int32, (half, half), 1))
        for part in range(2):
            here = pl.ds(part * half, half)
            qs = qb[h, here, :]
            diag = jnp.where(causal, dot(kb[h, here, :], qs, (1, 1)), -jnp.inf)
            top = jnp.max(diag, axis=0, keepdims=True)
            if part == 1:
                past = dot(kb[h, pl.ds(0, half), :], qs, (1, 1))
                top = jnp.maximum(top, jnp.max(past, axis=0, keepdims=True))
                past = jnp.exp2((past - top) * rate)
            diag = jnp.exp2((diag - top) * rate)
            total = jnp.sum(diag, axis=0, keepdims=True)
            if part == 1:
                total = total + jnp.sum(past, axis=0, keepdims=True)
            inverse = 1.0 / total
            out = dot(vt[h, pl.ds(0, width), here], (diag * inverse).astype(BF16), (1, 0))
            if part == 1:
                out = out + dot(vt[h, pl.ds(0, width), pl.ds(0, half)], (past * inverse).astype(BF16), (1, 0))
            loc[h, :, here] = out * keep

    def z_stage(h):
        @pl.when(z > 0)
        def _():
            for piece in pieces:
                part = piece[1]
                z_copy(plane_sum, h, piece).wait_recv()
                got = z_in[h, part, :]
                before[h, part, :] = before[h, part, :] + got

                @pl.when(z < z_size - 1)
                def _():
                    plane_sum[h, part, :] = plane_sum[h, part, :] + got
                    z_copy(plane_sum, h, piece).start()

    def read(h):
        share = 1.0 / (1.0 + jnp.exp(jnp.full((1, rows), -gate[h], F32)))
        lift_query = lifted(qb[h].astype(F32)).astype(BF16)
        norm = before[h, pl.ds(width, 1), :]
        high = norm.astype(BF16).astype(F32)
        middle = (norm - high).astype(BF16).astype(F32)
        low = norm - high - middle
        row = lax.broadcasted_iota(jnp.int32, (PAD, width), 0)
        parts = jnp.where(row == 0, high, jnp.where(row == 1, middle, jnp.where(row == 2, low, 0.0)))
        memory = before[h, pl.ds(0, width), :].astype(BF16)
        got = dot(jnp.concatenate([memory, parts.astype(BF16)], axis=0), lift_query, (1, 1))
        denominator = jnp.sum(got[width:width + 8], axis=0, keepdims=True)
        value = got[:width] * (share / jnp.maximum(denominator, 1.0)) + loc[h]
        attn[:, pl.ds(pl.multiple_of(h * width, width), width)] = value.astype(BF16).T

    def columns(n):
        return pl.ds(pl.multiple_of(n * tile, tile), tile)

    def project_first():
        load_w(0).wait()
        part = pl.ds(0, depth)

        def one(n, _):
            acc[n] = dot(attn[:, part], wb[part, columns(n)], (1, 0))
            return 0

        lax.fori_loop(0, tiles, one, 0)

    def update_pair(first):
        for h in (first, first + 1):
            load(k_hbm, kb, k_sem, h).wait()
            load(v_hbm, vb, v_sem, h).wait()
        for h in (first, first + 1):
            update(h)

    update_pair(0)
    x_line.begin(own, 0)
    x_line.begin(own, 1)
    lax.fori_loop(LEAD, heads, start_loads, 0)
    lax.fori_loop(0, heads, start_queries, 0)
    lax.fori_loop(0, groups, start_weights, 0)
    update_pair(2)
    x_line.begin(own, 2)
    x_line.begin(own, 3)
    update_pair(4)

    def within(h):
        return jnp.logical_and(h >= 0, h < heads)

    late = max(heads - 4, z_size + 1)
    read_lag = jnp.where(z == z_size - 1, z_size + 1, late)

    def step(t, _):
        even = lax.rem(t, 2) == 0

        @pl.when(t < heads)
        def _():
            x_line.finish(own, before, row_sum, t, False)
            y_line.begin(row_sum, t)

        @pl.when(t < heads - 4)
        def _():
            x_line.begin(own, t + 4)

        @pl.when(within(t - 2))
        def _():
            y_line.finish(row_sum, before, plane_sum, t - 2, True)

            @pl.when(z == 0)
            def _():
                for piece in pieces:
                    z_copy(plane_sum, t - 2, piece).start()

        h = t - 2 - z

        @pl.when(within(h))
        def _():
            z_stage(h)

        @pl.when(jnp.logical_and(even, t < heads))
        def _():
            for head in (t, t + 1):
                load(q_hbm, qb, q_sem, head).wait()
            for head in (t, t + 1):
                local(head)

        @pl.when(jnp.logical_and(jnp.logical_not(even), t < heads - LEAD))
        def _():
            update_pair(t + 5)

        ready = t - read_lag

        @pl.when(jnp.logical_and(within(ready), lax.rem(ready, 2) == 1))
        def _():
            read(ready - 1)
            read(ready)

            @pl.when(ready == GROUP - 1)
            def _():
                project_first()
        return 0

    lax.fori_loop(0, heads + late, step, 0)

    last = pl.ds((groups - 1) * depth, depth)
    load_w(groups - 1).wait()
    theirs = pl.ds(pl.multiple_of(other * half, half), half)
    mine = pl.ds(pl.multiple_of(core * half, half), half)

    def to_peer(n):
        return pltpu.make_async_remote_copy(
            acc.at[n, theirs, :], peer.at[n], peer_send.at[n], peer_recv.at[n],
            device_id=(seq, other), device_id_type=MESH)

    def result(n):
        return pltpu.make_async_copy(outb.at[:, columns(n)], o_hbm.at[:, columns(n)], o_sem.at[n])

    def send_tile(n, _):
        acc[n, theirs, :] = acc[n, theirs, :] + dot(attn[theirs, last], wb[last, columns(n)], (1, 0))
        to_peer(n).start()
        return 0

    def own_tile(n, _):
        value = acc[n, mine, :] + dot(attn[mine, last], wb[last, columns(n)], (1, 0))
        to_peer(n).wait_recv()
        outb[:, columns(n)] = (value + peer[n]).astype(BF16)
        result(n).start()
        return 0

    lax.fori_loop(0, tiles, send_tile, 0)
    lax.fori_loop(0, tiles, own_tile, 0)

    def drain(h, _):
        x_line.drain(own, h)
        y_line.drain(row_sum, h)

        @pl.when(z < z_size - 1)
        def _():
            for piece in pieces:
                z_copy(plane_sum, h, piece).wait_send()
        return 0

    def drain_tiles(n, _):
        to_peer(n).wait_send()
        result(n).wait()
        return 0

    lax.fori_loop(0, heads, drain, 0)
    lax.fori_loop(0, tiles, drain_tiles, 0)


def on_device(sizes, queries, keys, values, gate_bias, out_weight):
    heads = gate_bias.shape[0]
    rows, feat = queries.shape
    width = feat // heads
    model = out_weight.shape[1]
    tile = 512
    tiles = model // tile
    state = (width + 8, width)
    box = pltpu.VMEM((heads,) + state, F32)
    sem = pltpu.SemaphoreType.DMA((heads,))
    tile_sem = pltpu.SemaphoreType.DMA((tiles,))
    blocks = pltpu.VMEM((heads, rows, width), BF16)
    scratch = [
        blocks, blocks, blocks,
        pltpu.VMEM((heads, width + PAD, rows), BF16),
        pltpu.VMEM(out_weight.shape, BF16),
        pltpu.VMEM((heads, width, rows), F32),
        pltpu.VMEM((rows, feat), BF16),
        pltpu.VMEM((tiles, rows, tile), F32),
        pltpu.VMEM((tiles, rows // 2, tile), F32),
        pltpu.VMEM((rows // 2, model), BF16),
        box, box, box, box, box,
        sem, sem, sem, pltpu.SemaphoreType.DMA((heads // GROUP,)), tile_sem,
        pltpu.SemaphoreType.DMA((2, heads)), pltpu.SemaphoreType.DMA((2, heads)), tile_sem, tile_sem,
    ] + line_scratch(sizes[0], heads, state) + line_scratch(sizes[1], heads, state)
    hbm = pl.BlockSpec(memory_space=pl.ANY)
    return pl.pallas_call(
        functools.partial(kernel, sizes, tile),
        out_shape=jax.ShapeDtypeStruct((rows // 2, model), BF16),
        in_specs=[pl.BlockSpec(memory_space=pltpu.SMEM), hbm, hbm, hbm, hbm],
        out_specs=hbm,
        scratch_shapes=scratch,
        compiler_params=pltpu.CompilerParams(
            collective_id=0, has_side_effects=True, vmem_limit_bytes=62 * 1024 * 1024),
        cost_estimate=pl.CostEstimate(
            flops=2 * rows * feat * (model + rows + 2 * width), bytes_accessed=24 * 1024 * 1024,
            transcendentals=heads * rows * rows),
    )(gate_bias, queries, keys, values, out_weight)


def grid_of(count):
    z_size = min(4, count)
    plane = count // z_size
    y_size = 1
    while y_size * y_size < plane:
        y_size *= 2
    return (plane // y_size, y_size, z_size)


def solution(mesh):
    in_specs = (P("seq", "head"), P("seq", "head"), P("seq", "head"), P("head"), P("head", None))
    out_specs = P(("seq", "head"), None)
    return jax.shard_map(
        functools.partial(on_device, grid_of(mesh.shape["seq"])),
        mesh=mesh, in_specs=in_specs, out_specs=out_specs, check_vma=False
    )
```

```python
import functools

import jax
import jax.numpy as jnp
from jax import lax
from jax.experimental import pallas as pl
from jax.experimental.pallas import tpu as pltpu
from jax.sharding import PartitionSpec as P

SEG = 512
MESH = pl.DeviceIdType.MESH
F32 = jnp.float32
BF16 = jnp.bfloat16


def lifted(source):
    return jnp.where(source > 0, source + 1.0, jnp.exp(jnp.minimum(source, 0.0)))


def dot(a, b, dims):
    return lax.dot_general(a, b, ((dims[:1], dims[1:]), ((), ())), preferred_element_type=F32)


class Line:
    def __init__(self, size, place, device, refs):
        self.size, self.place, self.device = size, place, device
        if size == 2:
            self.inbox, self.send, self.recv = refs
        else:
            (self.right_in, self.left_in, self.right_out, self.left_out,
             self.right_send, self.right_recv, self.left_send, self.left_recv) = refs

    def swap(self, src, h):
        return pltpu.make_async_remote_copy(
            src.at[h], self.inbox.at[h], self.send.at[h], self.recv.at[h],
            device_id=self.device(1 - self.place), device_id_type=MESH)

    def to_right(self, src, h):
        return pltpu.make_async_remote_copy(
            src.at[h], self.right_in.at[h], self.right_send.at[h], self.right_recv.at[h],
            device_id=self.device(jnp.minimum(self.place + 1, self.size - 1)), device_id_type=MESH)

    def to_left(self, src, h):
        return pltpu.make_async_remote_copy(
            src.at[h], self.left_in.at[h], self.left_send.at[h], self.left_recv.at[h],
            device_id=self.device(jnp.maximum(self.place - 1, 0)), device_id_type=MESH)

    def begin(self, src, h):
        if self.size == 2:
            self.swap(src, h).start()
            return

        @pl.when(self.place == 0)
        def _():
            self.to_right(src, h).start()

        @pl.when(self.place == self.size - 1)
        def _():
            self.to_left(src, h).start()

    def finish(self, src, before, total, h, add):
        if self.size == 2:
            self.swap(src, h).wait_recv()
            got = self.inbox[h]
            total[h] = src[h] + got
            earlier = jnp.where(self.place > 0, got, jnp.zeros_like(got))
            before[h] = before[h] + earlier if add else earlier
            return
        place, last = self.place, self.size - 1
        total[h] = src[h]
        if not add:
            before[h] = jnp.zeros(before.shape[1:], F32)

        @pl.when(place > 0)
        def _():
            self.to_right(src, h).wait_recv()
            got = self.right_in[h]
            before[h] = before[h] + got
            total[h] = total[h] + got

            @pl.when(place < last)
            def _():
                self.right_out[h] = got + src[h]
                self.to_right(self.right_out, h).start()

        @pl.when(place < last)
        def _():
            self.to_left(src, h).wait_recv()
            got = self.left_in[h]
            total[h] = total[h] + got

            @pl.when(place > 0)
            def _():
                self.left_out[h] = got + src[h]
                self.to_left(self.left_out, h).start()

    def drain(self, src, h):
        if self.size == 2:
            self.swap(src, h).wait_send()
            return

        @pl.when(self.place < self.size - 1)
        def _():
            self.to_right(src, h).wait_send()

        @pl.when(self.place > 0)
        def _():
            self.to_left(src, h).wait_send()


def line_scratch(size, heads, state):
    box = pltpu.VMEM((heads,) + state, F32)
    sem = pltpu.SemaphoreType.DMA((heads,))
    return [box, sem, sem] if size == 2 else [box] * 4 + [sem] * 4


GROUP = 8
PAD = 16
LEAD = 6


def kernel(sizes, tile, gate, q_hbm, k_hbm, v_hbm, w_hbm, o_hbm, *scratch):
    x_size, y_size, z_size = sizes
    scratch = list(scratch)

    def take(count):
        taken = scratch[:count]
        del scratch[:count]
        return taken

    qb, kb, vb, vt, wb, loc, attn, acc, peer, outb = take(10)
    own, row_sum, plane_sum, before, z_in = take(5)
    q_sem, k_sem, v_sem, w_sem, o_sem = take(5)
    z_send, z_recv, peer_send, peer_recv = take(4)
    x_refs = take(3 if x_size == 2 else 8)
    y_refs = take(3 if y_size == 2 else 8)

    heads, rows, width = qb.shape
    half = rows // 2
    tiles = acc.shape[0]
    depth = GROUP * width
    groups = heads // GROUP
    seq, core = lax.axis_index("seq"), lax.axis_index("head")
    x = lax.rem(seq, x_size)
    y = lax.rem(seq // x_size, y_size)
    z = seq // (x_size * y_size)

    def at(xx, yy, zz):
        return ((zz * y_size + yy) * x_size + xx, core)

    x_line = Line(x_size, x, lambda c: at(c, y, z), x_refs)
    y_line = Line(y_size, y, lambda c: at(x, c, z), y_refs)
    other = 1 - core

    def load(src, dst, sem, h):
        return pltpu.make_async_copy(
            src.at[:, pl.ds(pl.multiple_of(h * width, width), width)], dst.at[h], sem.at[h])

    def load_w(g):
        part = pl.ds(pl.multiple_of(g * depth, depth), depth)
        return pltpu.make_async_copy(w_hbm.at[part, :], wb.at[part, :], w_sem.at[g])

    def start_loads(h, _):
        load(k_hbm, kb, k_sem, h).start()
        load(v_hbm, vb, v_sem, h).start()
        return 0

    def start_queries(h, _):
        load(q_hbm, qb, q_sem, h).start()
        return 0

    def start_weights(g, _):
        load_w(g).start()
        return 0

    lax.fori_loop(0, LEAD, start_loads, 0)

    barrier = pltpu.get_barrier_semaphore()
    pl.semaphore_signal(barrier, inc=1, device_id=(seq, other), device_id_type=MESH)
    greeted = 1
    for place, size, where in (
        (x, x_size, lambda c: at(c, y, z)),
        (y, y_size, lambda c: at(x, c, z)),
        (z, z_size, lambda c: at(x, y, c)),
    ):
        @pl.when(place > 0)
        def _():
            pl.semaphore_signal(barrier, inc=1, device_id=where(place - 1), device_id_type=MESH)

        @pl.when(place < size - 1)
        def _():
            pl.semaphore_signal(barrier, inc=1, device_id=where(place + 1), device_id_type=MESH)

        greeted = greeted + (place > 0).astype(jnp.int32) + (place < size - 1).astype(jnp.int32)
    pl.semaphore_wait(barrier, greeted)

    cut = width // 2
    pieces = ((0, pl.ds(0, cut)), (1, pl.ds(cut, width + 8 - cut)))

    def z_copy(src, h, piece):
        index, part = piece
        return pltpu.make_async_remote_copy(
            src.at[h, part, :], z_in.at[h, part, :], z_send.at[index, h], z_recv.at[index, h],
            device_id=at(x, y, jnp.minimum(z + 1, z_size - 1)), device_id_type=MESH)

    def update(h):
        lift_key = lifted(kb[h].astype(F32)).astype(BF16)
        vt[h, pl.ds(0, width), :] = vb[h].T
        vt[h, pl.ds(width, PAD), :] = jnp.ones((PAD, rows), BF16)
        own[h] = dot(vt[h], lift_key, (1, 0))[:width + 8]

    def local(h):
        rate = 1.4426950408889634 / (width ** 0.5)
        keep = 1.0 / (1.0 + jnp.exp(jnp.full((1, half), gate[h], F32)))
        causal = (lax.broadcasted_iota(jnp.int32, (half, half), 0)
                  <= lax.broadcasted_iota(jnp.int32, (half, half), 1))
        for part in range(2):
            here = pl.ds(part * half, half)
            qs = qb[h, here, :]
            diag = jnp.where(causal, dot(kb[h, here, :], qs, (1, 1)), -jnp.inf)
            top = jnp.max(diag, axis=0, keepdims=True)
            if part == 1:
                past = dot(kb[h, pl.ds(0, half), :], qs, (1, 1))
                top = jnp.maximum(top, jnp.max(past, axis=0, keepdims=True))
                past = jnp.exp2((past - top) * rate)
            diag = jnp.exp2((diag - top) * rate)
            total = jnp.sum(diag, axis=0, keepdims=True)
            if part == 1:
                total = total + jnp.sum(past, axis=0, keepdims=True)
            inverse = 1.0 / total
            out = dot(vt[h, pl.ds(0, width), here], (diag * inverse).astype(BF16), (1, 0))
            if part == 1:
                out = out + dot(vt[h, pl.ds(0, width), pl.ds(0, half)], (past * inverse).astype(BF16), (1, 0))
            loc[h, :, here] = out * keep

    def z_stage(h):
        @pl.when(z > 0)
        def _():
            for piece in pieces:
                part = piece[1]
                z_copy(plane_sum, h, piece).wait_recv()
                got = z_in[h, part, :]
                before[h, part, :] = before[h, part, :] + got

                @pl.when(z < z_size - 1)
                def _():
                    plane_sum[h, part, :] = plane_sum[h, part, :] + got
                    z_copy(plane_sum, h, piece).start()

    def read(h):
        share = 1.0 / (1.0 + jnp.exp(jnp.full((1, rows), -gate[h], F32)))
        lift_query = lifted(qb[h].astype(F32)).astype(BF16)
        norm = before[h, pl.ds(width, 1), :]
        high = norm.astype(BF16).astype(F32)
        middle = (norm - high).astype(BF16).astype(F32)
        low = norm - high - middle
        row = lax.broadcasted_iota(jnp.int32, (PAD, width), 0)
        parts = jnp.where(row == 0, high, jnp.where(row == 1, middle, jnp.where(row == 2, low, 0.0)))
        memory = before[h, pl.ds(0, width), :].astype(BF16)
        got = dot(jnp.concatenate([memory, parts.astype(BF16)], axis=0), lift_query, (1, 1))
        denominator = jnp.sum(got[width:width + 8], axis=0, keepdims=True)
        value = got[:width] * (share / jnp.maximum(denominator, 1.0)) + loc[h]
        attn[:, pl.ds(pl.multiple_of(h * width, width), width)] = value.astype(BF16).T

    def columns(n):
        return pl.ds(pl.multiple_of(n * tile, tile), tile)

    per_step = tiles // (heads - GROUP)
    assert per_step * (heads - GROUP) == tiles

    def project_first(n):
        part = pl.ds(0, depth)
        acc[n] = dot(attn[:, part], wb[part, columns(n)], (1, 0))

    def update_pair(first):
        for h in (first, first + 1):
            load(k_hbm, kb, k_sem, h).wait()
            load(v_hbm, vb, v_sem, h).wait()
        for h in (first, first + 1):
            update(h)

    update_pair(0)
    x_line.begin(own, 0)
    x_line.begin(own, 1)
    lax.fori_loop(LEAD, heads, start_loads, 0)
    lax.fori_loop(0, heads, start_queries, 0)
    lax.fori_loop(0, groups, start_weights, 0)
    update_pair(2)
    x_line.begin(own, 2)
    x_line.begin(own, 3)
    update_pair(4)

    def within(h):
        return jnp.logical_and(h >= 0, h < heads)

    late = max(heads - 4, z_size + 1)
    read_lag = jnp.where(z == z_size - 1, z_size + 1, late - 2 * z)

    def step(t, _):
        even = lax.rem(t, 2) == 0

        @pl.when(t < heads)
        def _():
            x_line.finish(own, before, row_sum, t, False)
            y_line.begin(row_sum, t)

        @pl.when(t < heads - 4)
        def _():
            x_line.begin(own, t + 4)

        @pl.when(within(t - 2))
        def _():
            y_line.finish(row_sum, before, plane_sum, t - 2, True)

            @pl.when(z == 0)
            def _():
                for piece in pieces:
                    z_copy(plane_sum, t - 2, piece).start()

        h = t - 2 - z

        @pl.when(within(h))
        def _():
            z_stage(h)

        @pl.when(jnp.logical_and(even, t < heads))
        def _():
            for head in (t, t + 1):
                load(q_hbm, qb, q_sem, head).wait()
            for head in (t, t + 1):
                local(head)

        @pl.when(jnp.logical_and(jnp.logical_not(even), t < heads - LEAD))
        def _():
            update_pair(t + 5)

        ready = t - read_lag

        @pl.when(jnp.logical_and(within(ready), lax.rem(ready, 2) == 1))
        def _():
            read(ready - 1)
            read(ready)

            @pl.when(ready == GROUP - 1)
            def _():
                load_w(0).wait()

        @pl.when(jnp.logical_and(ready >= GROUP, ready < heads))
        def _():
            for piece in range(per_step):
                project_first((ready - GROUP) * per_step + piece)
        return 0

    lax.fori_loop(0, heads + late, step, 0)

    last = pl.ds((groups - 1) * depth, depth)
    load_w(groups - 1).wait()
    theirs = pl.ds(pl.multiple_of(other * half, half), half)
    mine = pl.ds(pl.multiple_of(core * half, half), half)

    def to_peer(n):
        return pltpu.make_async_remote_copy(
            acc.at[n, theirs, :], peer.at[n], peer_send.at[n], peer_recv.at[n],
            device_id=(seq, other), device_id_type=MESH)

    def result(n):
        return pltpu.make_async_copy(outb.at[:, columns(n)], o_hbm.at[:, columns(n)], o_sem.at[n])

    def send_tile(n, _):
        acc[n, theirs, :] = acc[n, theirs, :] + dot(attn[theirs, last], wb[last, columns(n)], (1, 0))
        to_peer(n).start()
        return 0

    def own_tile(n, _):
        value = acc[n, mine, :] + dot(attn[mine, last], wb[last, columns(n)], (1, 0))
        to_peer(n).wait_recv()
        outb[:, columns(n)] = (value + peer[n]).astype(BF16)
        result(n).start()
        return 0

    lax.fori_loop(0, tiles, send_tile, 0)
    lax.fori_loop(0, tiles, own_tile, 0)

    def drain(h, _):
        x_line.drain(own, h)
        y_line.drain(row_sum, h)

        @pl.when(z < z_size - 1)
        def _():
            for piece in pieces:
                z_copy(plane_sum, h, piece).wait_send()
        return 0

    def drain_tiles(n, _):
        to_peer(n).wait_send()
        result(n).wait()
        return 0

    lax.fori_loop(0, heads, drain, 0)
    lax.fori_loop(0, tiles, drain_tiles, 0)


def on_device(sizes, queries, keys, values, gate_bias, out_weight):
    heads = gate_bias.shape[0]
    rows, feat = queries.shape
    width = feat // heads
    model = out_weight.shape[1]
    tile = 512
    tiles = model // tile
    state = (width + 8, width)
    box = pltpu.VMEM((heads,) + state, F32)
    sem = pltpu.SemaphoreType.DMA((heads,))
    tile_sem = pltpu.SemaphoreType.DMA((tiles,))
    blocks = pltpu.VMEM((heads, rows, width), BF16)
    scratch = [
        blocks, blocks, blocks,
        pltpu.VMEM((heads, width + PAD, rows), BF16),
        pltpu.VMEM(out_weight.shape, BF16),
        pltpu.VMEM((heads, width, rows), F32),
        pltpu.VMEM((rows, feat), BF16),
        pltpu.VMEM((tiles, rows, tile), F32),
        pltpu.VMEM((tiles, rows // 2, tile), F32),
        pltpu.VMEM((rows // 2, model), BF16),
        box, box, box, box, box,
        sem, sem, sem, pltpu.SemaphoreType.DMA((heads // GROUP,)), tile_sem,
        pltpu.SemaphoreType.DMA((2, heads)), pltpu.SemaphoreType.DMA((2, heads)), tile_sem, tile_sem,
    ] + line_scratch(sizes[0], heads, state) + line_scratch(sizes[1], heads, state)
    hbm = pl.BlockSpec(memory_space=pl.ANY)
    return pl.pallas_call(
        functools.partial(kernel, sizes, tile),
        out_shape=jax.ShapeDtypeStruct((rows // 2, model), BF16),
        in_specs=[pl.BlockSpec(memory_space=pltpu.SMEM), hbm, hbm, hbm, hbm],
        out_specs=hbm,
        scratch_shapes=scratch,
        compiler_params=pltpu.CompilerParams(
            collective_id=0, has_side_effects=True, vmem_limit_bytes=62 * 1024 * 1024),
        cost_estimate=pl.CostEstimate(
            flops=2 * rows * feat * (model + rows + 2 * width), bytes_accessed=24 * 1024 * 1024,
            transcendentals=heads * rows * rows),
    )(gate_bias, queries, keys, values, out_weight)


def grid_of(count):
    z_size = min(4, count)
    plane = count // z_size
    y_size = 1
    while y_size * y_size < plane:
        y_size *= 2
    return (plane // y_size, y_size, z_size)


def solution(mesh):
    in_specs = (P("seq", "head"), P("seq", "head"), P("seq", "head"), P("head"), P("head", None))
    out_specs = P(("seq", "head"), None)
    return jax.shard_map(
        functools.partial(on_device, grid_of(mesh.shape["seq"])),
        mesh=mesh, in_specs=in_specs, out_specs=out_specs, check_vma=False
    )
```
